512 devices in a mesh: section: 16 (over z), frame: 32 (over x, y, core).
Axes of the slice: x: 4, y: 4, z: 16, core: 2. Of those that a mesh axis runs over, the one named last changes fastest.
Arguments:
- inflow: bfloat16 [128, 4096], P(None, 'frame'), may hold values from -6 to 6
- gains: bfloat16 [16, 4096], P('section'), may hold values from 0.25 to 1.75
- w_query: bfloat16 [16, 4096, 4096], P('section', None, 'frame'), may hold values from -1 to 1
- w_key: bfloat16 [16, 4096, 4096], P('section', None, 'frame'), may hold values from -0.046875 to 0.046875
- w_value: bfloat16 [16, 4096, 4096], P('section', None, 'frame'), may hold values from -0.046875 to 0.046875
- cache_keys: bfloat16 [16, 256, 4096], P('section', None, 'frame'), may hold values from -6 to 6
- cache_values: bfloat16 [16, 256, 4096], P('section', None, 'frame'), may hold values from -6 to 6
- w_depth_in: bfloat16 [4096, 1024], P(None, 'section'), may hold values from -0.046875 to 0.046875
- code_table: bfloat16 [2048, 1024], P(None, 'section'), may hold values from -6 to 6
- w_dquery: bfloat16 [1024, 1024], P(None, 'section'), may hold values from -1 to 1
- w_dkey: bfloat16 [1024, 1024], P(None, 'section'), may hold values from -1 to 1
- w_dvalue: bfloat16 [1024, 1024], P(None, 'section'), may hold values from -0.1875 to 0.1875
- w_dout: bfloat16 [1024, 1024], P('section'), may hold values from -0.1875 to 0.1875
- codes: int32 [128, 7], P('frame'), may hold values from 0 to 2047
- speaker_mask: int32 [128], P('frame'), may hold values 0 or 1
- cotangent: bfloat16 [128, 8, 1024], P('frame', None, 'section'), may hold values from -6 to 6
Outputs:
- new_keys: bfloat16 [16, 128, 4096], P('section', None, 'frame')
- new_values: bfloat16 [16, 128, 4096], P('section', None, 'frame')
- depth_out: bfloat16 [128, 8, 1024], P('frame', None, 'section')
- temporal_grad: bfloat16 [128, 4096], P('frame', 'section')
The draws below stay inside these ranges and needn't reach their ends.
All inputs are finite; a program needn't handle non-finite values. No bound on the sum of `speaker_mask` on one device may be relied on, other than what follows from the above.
Results may differ from the reference program's by a relative error of at most 0.038.
Values may be sent and summed in bfloat16 or wider, within the bound.
No kernel may reach another device: no remote copies, remote signals or barrier semaphores. Data moves between devices by JAX's collectives and lax.ppermute only.
A program may use at most 64 MiB of HBM per device.

```python
import jax
import jax.numpy as jnp
from jax import lax

D = 4096
HEADS = 32
CH = 64
STRETCHES = 2
CACHE = 256
DD = 1024
DHEADS = 16
LEVELS = 8
VOCAB = 2048
LAYERS = 16
FRAMES = 128
N_SECTION = 16


def draw_inflow(key, part):
    key = jax.random.fold_in(key, 1)
    values = jnp.clip(jax.random.normal(key, (FRAMES, D), jnp.float32), -6.0, 6.0)
    return values.astype(jnp.bfloat16)


def draw_w_query(key, part):
    key = jax.random.fold_in(key, 2)
    layer_keys = jax.random.split(key, LAYERS)

    def one_layer(layer_key):
        normal_part = jnp.clip(jax.random.normal(layer_key, (D, D), jnp.float32), -6.0, 6.0)
        return (normal_part * D ** (-0.5)).astype(jnp.bfloat16)
    return lax.map(one_layer, layer_keys)


def draw_cache_keys(key, part):
    key = jax.random.fold_in(key, 3)
    values = jnp.clip(jax.random.normal(key, (LAYERS, CACHE, D), jnp.float32), -6.0, 6.0)
    return values.astype(jnp.bfloat16)


def draw_code_table(key, part):
    key = jax.random.fold_in(key, 4)
    values = jnp.clip(jax.random.normal(key, (VOCAB, DD), jnp.float32), -6.0, 6.0)
    return values.astype(jnp.bfloat16)


def draw_w_dquery(key, part):
    key = jax.random.fold_in(key, 5)
    values = jnp.clip(jax.random.normal(key, (DD, DD), jnp.float32), -6.0, 6.0) * DD ** (-0.5)
    return values.astype(jnp.bfloat16)


def draw_w_dkey(key, part):
    key = jax.random.fold_in(key, 6)
    values = jnp.clip(jax.random.normal(key, (DD, DD), jnp.float32), -6.0, 6.0) * DD ** (-0.5)
    return values.astype(jnp.bfloat16)


def with_ends(entries, own_key, least, top_value):
    index_at = [jax.random.randint(jax.random.fold_in(own_key, axis), (), 0, length) for axis, length in enumerate(entries.shape)]
    longest = entries.shape.index(max(entries.shape))
    next_to = index_at[:longest] + [(index_at[longest] + 1) % entries.shape[longest]] + index_at[longest + 1:]
    return entries.at[tuple(index_at)].set(least).at[tuple(next_to)].set(top_value)


def shard_levels(rng, dims, cuts, smallest, largest):
    level, own = 1.0, jax.random.fold_in(rng, 6)
    for axis_at, shards_of in cuts:
        heights = jnp.exp(jax.random.uniform(jax.random.fold_in(own, axis_at), (shards_of,), jnp.float32, smallest / len(cuts), largest / len(cuts)))
        level = level * jnp.repeat(heights, dims[axis_at] // shards_of).reshape([-1 if axis == axis_at else 1 for axis in range(len(dims))])
    return level


def normal_values(stream_key, dims, deviation, most, cuts=(), held_as=jnp.bfloat16):
    result = jax.random.normal(stream_key, dims, jnp.float32) * deviation
    if len(cuts) > 0:
        result = shard_levels(stream_key, dims, cuts, -0.22, 0.18) * result
    return jnp.clip(result, min=-most, max=most).astype(held_as)


def setup_inputs(seed: int = 0) -> dict:
    streams_of = jax.random.split(jax.random.key(seed), 17)
    return {
        "inflow": draw_inflow(jax.random.fold_in(streams_of[16], 71), 0),
        "gains": jnp.clip(1.0 + 0.15 * jax.random.normal(streams_of[1], (LAYERS, D), jnp.float32), 0.25, 1.75).astype(jnp.bfloat16),
        "w_query": draw_w_query(jax.random.fold_in(streams_of[16], 71), 0),
        "w_key": normal_values(streams_of[3], (LAYERS, D, D), (4 * D) ** -0.5, 0.046875, ((0, 16), (2, 32))),
        "w_value": normal_values(streams_of[4], (LAYERS, D, D), (4 * D) ** -0.5, 0.046875, ((0, 16), (2, 32))),
        "cache_keys": draw_cache_keys(jax.random.fold_in(streams_of[16], 71), 0),
        "cache_values": normal_values(streams_of[6], (LAYERS, CACHE, D), 1.0, 6.0, ((0, 16), (2, 32))),
        "w_depth_in": normal_values(streams_of[7], (D, DD), (4 * D) ** -0.5, 0.046875, ((1, 16),)),
        "code_table": draw_code_table(jax.random.fold_in(streams_of[16], 71), 0),
        "w_dquery": draw_w_dquery(jax.random.fold_in(streams_of[16], 71), 0),
        "w_dkey": draw_w_dkey(jax.random.fold_in(streams_of[16], 71), 0),
        "w_dvalue": normal_values(streams_of[11], (DD, DD), DD ** -0.5, 0.1875, ((1, 16),)),
        "w_dout": normal_values(streams_of[12], (DD, DD), DD ** -0.5, 0.1875, ((0, 16),)),
        "codes": with_ends(jax.random.randint(streams_of[13], (FRAMES, LEVELS - 1), 0, VOCAB), jax.random.fold_in(streams_of[13], 1), 0, VOCAB - 1).astype(jnp.int32),
        "speaker_mask": with_ends((jax.random.randint(streams_of[14], (FRAMES,), 0, 4) < 3).astype(jnp.int32), jax.random.fold_in(streams_of[14], 1), 0, 1),
        "cotangent": normal_values(streams_of[15], (FRAMES, LEVELS, DD), 1.0, 6.0, ((0, 32), (2, 16))),
    }


EPSILON = 1e-05
MASKED = -1e+30

def block_attention(query, keys, values, start, heads):
    rows, width = query.shape
    size = width // heads
    query3 = query.reshape(rows, heads, size).astype(jnp.float32)
    keys3 = keys.reshape(-1, heads, size).astype(jnp.float32)
    values3 = values.reshape(-1, heads, size).astype(jnp.float32)
    scores = jnp.einsum('qhd,khd->hqk', query3, keys3) * size ** (-0.5)
    allowed = jnp.arange(keys.shape[0])[None, :] <= start + jnp.arange(rows)[:, None]
    scores = jnp.where(allowed[None], scores, MASKED)
    peak = lax.optimization_barrier(jnp.max(scores, axis=-1, keepdims=True))
    raised = jnp.exp(scores - peak)
    probs = (raised / lax.optimization_barrier(jnp.sum(raised, axis=-1, keepdims=True))).astype(jnp.bfloat16)
    mixed = jnp.einsum('hqk,khd->qhd', probs.astype(jnp.float32), values3)
    return mixed.reshape(rows, width)

def level_attention(query, keys, values, heads):
    frames, levels, width = query.shape
    size = width // heads
    query4 = query.reshape(frames, levels, heads, size)
    keys4 = keys.reshape(frames, levels, heads, size)
    values4 = values.reshape(frames, levels, heads, size)
    scores = jnp.einsum('fqhd,fkhd->fhqk', query4, keys4, precision=lax.Precision.HIGHEST) * size ** (-0.5)
    causal = jnp.arange(levels)[:, None] >= jnp.arange(levels)[None, :]
    scores = jnp.where(causal, scores, MASKED)
    peak = lax.optimization_barrier(jnp.max(scores, axis=-1, keepdims=True))
    raised = jnp.exp(scores - peak)
    probs = raised / lax.optimization_barrier(jnp.sum(raised, axis=-1, keepdims=True))
    mixed = jnp.einsum('fhqk,fkhd->fqhd', probs, values4, precision=lax.Precision.HIGHEST)
    return (mixed.reshape(frames, levels, width), probs)

def level_attention_grad(grad_mixed, probs, query, keys, values, heads):
    frames, levels, width = query.shape
    size = width // heads
    query4 = query.reshape(frames, levels, heads, size)
    keys4 = keys.reshape(frames, levels, heads, size)
    values4 = values.reshape(frames, levels, heads, size)
    grad4 = grad_mixed.reshape(frames, levels, heads, size)
    high = lax.Precision.HIGHEST
    grad_values = jnp.einsum('fhqk,fqhd->fkhd', probs, grad4, precision=high)
    grad_probs = jnp.einsum('fqhd,fkhd->fhqk', grad4, values4, precision=high)
    inner = lax.optimization_barrier(jnp.sum(grad_probs * probs, axis=-1, keepdims=True))
    grad_scores = probs * (grad_probs - inner) * size ** (-0.5)
    grad_query = jnp.einsum('fhqk,fkhd->fqhd', grad_scores, keys4, precision=high)
    grad_keys = jnp.einsum('fhqk,fqhd->fkhd', grad_scores, query4, precision=high)
    shape = (frames, levels, width)
    return (grad_query.reshape(shape), grad_keys.reshape(shape), grad_values.reshape(shape))

def reference(inflow, gains, w_query, w_key, w_value, cache_keys, cache_values, w_depth_in, code_table, w_dquery, w_dkey, w_dvalue, w_dout, codes, speaker_mask, cotangent):
    high = lax.Precision.HIGHEST
    blocks = [inflow[b * CH:(b + 1) * CH] for b in range(STRETCHES)]
    keys_all = []
    values_all = []
    for layer in range(N_SECTION):
        key_list = []
        value_list = []
        outputs = []
        for b in range(STRETCHES):
            wide = blocks[b].astype(jnp.float32)
            scale_rows = lax.rsqrt(lax.optimization_barrier(jnp.mean(wide * wide, axis=1, keepdims=True)) + EPSILON)
            normed = (wide * scale_rows * gains[layer].astype(jnp.float32)).astype(jnp.bfloat16)
            query = jnp.dot(normed, w_query[layer], preferred_element_type=jnp.float32).astype(jnp.bfloat16)
            key_new = jnp.dot(normed, w_key[layer], preferred_element_type=jnp.float32).astype(jnp.bfloat16)
            value_new = jnp.dot(normed, w_value[layer], preferred_element_type=jnp.float32).astype(jnp.bfloat16)
            key_list.append(key_new)
            value_list.append(value_new)
            visible_keys = jnp.concatenate([cache_keys[layer]] + key_list, axis=0)
            visible_values = jnp.concatenate([cache_values[layer]] + value_list, axis=0)
            attended = block_attention(query, visible_keys, visible_values, CACHE + b * CH, HEADS)
            outputs.append((wide + attended).astype(jnp.bfloat16))
        blocks = outputs
        keys_all.append(jnp.concatenate(key_list, axis=0))
        values_all.append(jnp.concatenate(value_list, axis=0))
    new_keys = jnp.stack(keys_all, axis=0)
    new_values = jnp.stack(values_all, axis=0)
    temporal = jnp.concatenate(blocks, axis=0)
    base = jnp.dot(temporal, w_depth_in, preferred_element_type=jnp.float32)
    looked = code_table[codes].astype(jnp.float32)
    depth_in = jnp.concatenate([base[:, None, :], base[:, None, :] + looked], axis=1).astype(jnp.bfloat16)
    depth_wide = depth_in.astype(jnp.float32)
    dquery = jnp.einsum('fld,de->fle', depth_wide, w_dquery.astype(jnp.float32), precision=high)
    dkey = jnp.einsum('fld,de->fle', depth_wide, w_dkey.astype(jnp.float32), precision=high)
    dvalue = jnp.einsum('fld,de->fle', depth_wide, w_dvalue.astype(jnp.float32), precision=high)
    mixed, dprobs = level_attention(dquery, dkey, dvalue, DHEADS)
    mixed_low = mixed.astype(jnp.bfloat16)
    projected = jnp.einsum('fld,de->fle', mixed_low.astype(jnp.float32), w_dout.astype(jnp.float32), precision=high)
    depth_out = (depth_wide + projected).astype(jnp.bfloat16)
    grad_out = cotangent.astype(jnp.float32) * speaker_mask.astype(jnp.float32)[:, None, None]
    grad_low = grad_out.astype(jnp.bfloat16).astype(jnp.float32)
    grad_mixed = jnp.einsum('fle,de->fld', grad_low, w_dout.astype(jnp.float32), precision=high)
    grad_dquery, grad_dkey, grad_dvalue = level_attention_grad(grad_mixed, dprobs, dquery, dkey, dvalue, DHEADS)
    grad_dquery = grad_dquery.astype(jnp.bfloat16).astype(jnp.float32)
    grad_dkey = grad_dkey.astype(jnp.bfloat16).astype(jnp.float32)
    grad_dvalue = grad_dvalue.astype(jnp.bfloat16).astype(jnp.float32)
    grad_depth = grad_out + jnp.einsum('fle,de->fld', grad_dquery, w_dquery.astype(jnp.float32), precision=high)
    grad_depth = grad_depth + jnp.einsum('fle,de->fld', grad_dkey, w_dkey.astype(jnp.float32), precision=high)
    grad_depth = grad_depth + jnp.einsum('fle,de->fld', grad_dvalue, w_dvalue.astype(jnp.float32), precision=high)
    grad_base = lax.optimization_barrier(jnp.sum(grad_depth, axis=1)).astype(jnp.bfloat16)
    temporal_grad = jnp.dot(grad_base, w_depth_in.T, preferred_element_type=jnp.float32).astype(jnp.bfloat16)
    return (new_keys, new_values, depth_out, temporal_grad)
```

```python
import functools

import jax
import jax.numpy as jnp
from jax import lax
from jax.experimental import pallas as pl
from jax.experimental.pallas import tpu as pltpu
from jax.sharding import PartitionSpec as P

HEAD = 128
CH = 64
CACHE = 256
DHEAD = 64
SECTIONS = 16
CHIPS = 16
TICKS = SECTIONS + 2
PIECES = 8

EPSILON = 1e-05
MASKED = -1e30
BOTH = ("section", "frame")


def device_id(section, chip, core):
    return (section % SECTIONS) * 2 * CHIPS + chip * 2 + core


def plane_pairs(first):
    return [
        [device_id(low + up, chip, core) for up in range(2) for chip in range(CHIPS)]
        for low in range(first, SECTIONS, 2)
        for core in range(2)
    ]


def core_pairs():
    return [
        [device_id(section, chip, core) for core in range(2)]
        for section in range(SECTIONS)
        for chip in range(CHIPS)
    ]


def layer_kernel(
    where_ref,
    rows_ref,
    weight_ref,
    stash_k_ref,
    stash_v_ref,
    prev_k_ref,
    prev_v_ref,
    new_k_ref,
    new_v_ref,
    send_ref,
    held,
    arrived,
):
    depth = held.shape[0] // PIECES
    copies = []
    for piece in range(PIECES):
        span = pl.ds(piece * depth, depth)
        copy = pltpu.make_async_copy(weight_ref.at[span], held.at[span], arrived.at[piece])
        copy.start()
        copies.append(copy)
    block = where_ref[0]
    chip = where_ref[1]
    core = where_ref[2]
    total = jnp.zeros((CH, 3 * HEAD), jnp.float32)
    squares = jnp.zeros((CH, 2 * HEAD), jnp.float32)
    per_piece = CHIPS // PIECES
    for piece in range(PIECES):
        parts = []
        for at in range(piece * per_piece, (piece + 1) * per_piece):
            part = jnp.concatenate([rows_ref[0, at], rows_ref[1, at]], axis=1)
            wide = part.astype(jnp.float32)
            squares = squares + wide * wide
            parts.append(part)
        copies[piece].wait()
        total = total + jnp.dot(
            jnp.concatenate(parts, axis=1),
            held[pl.ds(piece * depth, depth), :],
            preferred_element_type=jnp.float32,
        )
    scale_rows = lax.rsqrt(
        jnp.sum(squares, axis=1, keepdims=True) * (1.0 / (2 * CHIPS * HEAD)) + EPSILON
    )
    projected = (total * scale_rows).astype(jnp.bfloat16)
    query = projected[:, :HEAD]
    key_new = projected[:, HEAD : 2 * HEAD]
    value_new = projected[:, 2 * HEAD :]
    new_k_ref[...] = key_new
    new_v_ref[...] = value_new
    keys = jnp.concatenate([stash_k_ref[...], prev_k_ref[...], key_new], axis=0)
    values = jnp.concatenate([stash_v_ref[...], prev_v_ref[...], value_new], axis=0)
    scores = lax.dot_general(
        query, keys, (((1,), (1,)), ((), ())), preferred_element_type=jnp.float32
    ) * HEAD ** (-0.5)
    at_key = lax.broadcasted_iota(jnp.int32, scores.shape, 1)
    at_row = lax.broadcasted_iota(jnp.int32, scores.shape, 0)
    old = jnp.where(block > 0, CACHE + CH, CACHE)
    allowed = (at_key < old) | ((at_key >= CACHE + CH) & (at_key - (CACHE + CH) <= at_row))
    scores = jnp.where(allowed, scores, MASKED)
    peak = jnp.max(scores, axis=-1, keepdims=True)
    raised = jnp.exp(scores - peak)
    probs = (raised / jnp.sum(raised, axis=-1, keepdims=True)).astype(jnp.bfloat16)
    attended = jnp.dot(probs, values, preferred_element_type=jnp.float32)
    own = rows_ref[core, chip].astype(jnp.float32)
    x_out = (own + attended).astype(jnp.bfloat16)
    for at in range(send_ref.shape[0]):
        send_ref[at] = x_out


def layer_step(where, rows, weight, stash_k, stash_v, prev_k, prev_v):
    vmem = pl.BlockSpec(memory_space=pltpu.VMEM)
    block = jax.ShapeDtypeStruct((CH, HEAD), jnp.bfloat16)
    return pl.pallas_call(
        layer_kernel,
        out_shape=(block, block, jax.ShapeDtypeStruct((2 * CHIPS, CH, HEAD), jnp.bfloat16)),
        in_specs=[
            pl.BlockSpec(memory_space=pltpu.SMEM),
            vmem,
            pl.BlockSpec(memory_space=pl.ANY),
            vmem,
            vmem,
            vmem,
            vmem,
        ],
        out_specs=(vmem, vmem, vmem),
        scratch_shapes=[
            pltpu.VMEM(weight.shape, jnp.bfloat16),
            pltpu.SemaphoreType.DMA((PIECES,)),
        ],
        compiler_params=pltpu.CompilerParams(vmem_limit_bytes=16 * 1024 * 1024),
        cost_estimate=pl.CostEstimate(
            flops=2 * CH * weight.size, bytes_accessed=2 * weight.size, transcendentals=0
        ),
    )(where, rows, weight, stash_k, stash_v, prev_k, prev_v)


def contract_last(a, b):
    return lax.dot_general(a, b, (((1,), (1,)), ((), ())), preferred_element_type=jnp.float32)


def depth_forward(z, whole, in_head, frames, levels):
    width = z.shape[1]
    high = lax.Precision.HIGHEST
    heads = in_head.shape[1]
    query, key, value = (
        contract_last(z, whole[at]).reshape(frames, levels, width) for at in range(3)
    )
    pairs = (query[:, :, None, :] * key[:, None, :, :]).reshape(-1, width)
    scores = jnp.dot(pairs, in_head, precision=high).reshape(frames, levels, levels, heads)
    scores = scores * DHEAD ** (-0.5)
    causal = jnp.arange(levels)[:, None] >= jnp.arange(levels)[None, :]
    scores = jnp.where(causal[None, :, :, None], scores, MASKED)
    peak = jnp.max(scores, axis=2, keepdims=True)
    raised = jnp.exp(scores - peak)
    probs = raised / jnp.sum(raised, axis=2, keepdims=True)
    spread = jnp.dot(probs.reshape(-1, heads), in_head.T, precision=high).reshape(
        frames, levels, levels, width
    )
    mixed = jnp.sum(spread * value[:, None, :, :], axis=2)
    return query, key, value, probs, spread, mixed


def depth_backward(grad_mixed, query, key, value, probs, spread, in_head):
    frames, levels, width = query.shape
    heads = in_head.shape[1]
    high = lax.Precision.HIGHEST
    grad_value = jnp.sum(spread * grad_mixed[:, :, None, :], axis=1)
    pairs = (grad_mixed[:, :, None, :] * value[:, None, :, :]).reshape(-1, width)
    grad_probs = jnp.dot(pairs, in_head, precision=high).reshape(probs.shape)
    inner = jnp.sum(grad_probs * probs, axis=2, keepdims=True)
    grad_scores = probs * (grad_probs - inner) * DHEAD ** (-0.5)
    wide = jnp.dot(grad_scores.reshape(-1, heads), in_head.T, precision=high).reshape(
        frames, levels, levels, width
    )
    grad_query = jnp.sum(wide * key[:, None, :, :], axis=2)
    grad_key = jnp.sum(wide * query[:, :, None, :], axis=1)
    return grad_query, grad_key, grad_value


def body(
    inflow,
    gains,
    w_query,
    w_key,
    w_value,
    cache_keys,
    cache_values,
    w_depth_in,
    code_table,
    w_dquery,
    w_dkey,
    w_dvalue,
    w_dout,
    codes,
    speaker_mask,
    cotangent,
):
    section_id = lax.axis_index("section")
    frame_id = lax.axis_index("frame")
    frames, levels, part = cotangent.shape
    width = part * SECTIONS
    features = w_depth_in.shape[0]

    looked = jnp.take(code_table, codes, axis=0).reshape(-1, part)
    masked = cotangent.astype(jnp.float32) * speaker_mask.astype(jnp.float32)[:, None, None]
    masked = masked.astype(jnp.bfloat16).reshape(-1, part)
    extra = jnp.concatenate([looked, masked], axis=0)
    extra = jnp.pad(extra, ((0, HEAD - extra.shape[0]), (0, 0)))
    shares = jnp.concatenate(
        [w_depth_in.T, w_dquery.T, w_dkey.T, w_dvalue.T, w_dout, extra.T], axis=1
    )
    shares = lax.all_gather(shares, "section", axis=0, tiled=True)

    gain = gains[0].astype(jnp.float32)[:, None]
    weight = jnp.concatenate([w_query[0], w_key[0], w_value[0]], axis=1)
    weight = (weight.astype(jnp.float32) * gain).astype(jnp.bfloat16)
    stash_k, stash_v = cache_keys[0], cache_values[0]

    def spread_out(block):
        return jnp.broadcast_to(block[None], (2 * CHIPS,) + block.shape)

    blank = jnp.zeros((CH, HEAD), jnp.bfloat16)
    keys, values, outs = [], [], []
    send = spread_out(inflow[:CH])
    for tick in range(TICKS):
        if tick == 2:
            send = jnp.where(section_id == SECTIONS - 1, spread_out(inflow[CH:]), send)
        first = 0 if tick == 0 else (tick - 1) % 2
        got = lax.all_to_all(
            send, BOTH, split_axis=0, concat_axis=0, tiled=True, axis_index_groups=plane_pairs(first)
        )[:CHIPS]
        rows = lax.all_gather(got, BOTH, axis=0, axis_index_groups=core_pairs())
        where = jnp.stack([tick - section_id, frame_id // 2, frame_id % 2]).astype(jnp.int32)
        new_k, new_v, send = layer_step(
            where,
            rows,
            weight,
            stash_k,
            stash_v,
            keys[tick - 2] if tick >= 2 else blank,
            values[tick - 2] if tick >= 2 else blank,
        )
        keys.append(new_k)
        values.append(new_v)
        outs.append(send)

    def in_order(found):
        stacked = jnp.stack(found)
        early = lax.dynamic_index_in_dim(stacked, section_id, 0, keepdims=False)
        late = lax.dynamic_index_in_dim(stacked, section_id + 2, 0, keepdims=False)
        return jnp.concatenate([early, late], axis=0)

    new_keys, new_values = in_order(keys), in_order(values)

    finished = jnp.concatenate([outs[TICKS - 3][0], outs[TICKS - 1][0]], axis=0)
    finished = finished.reshape(2 * CHIPS, frames, HEAD)
    temporal = lax.all_to_all(finished, "frame", split_axis=0, concat_axis=0, tiled=True)
    temporal = temporal.transpose(1, 0, 2).reshape(frames, features)
    w_in = shares[:, :features]
    whole = [
        shares[:, features + at * width : features + (at + 1) * width] for at in range(4)
    ]
    extra = shares[:, features + 4 * width :].T
    looked = extra[: frames * (levels - 1)].reshape(frames, levels - 1, width)
    masked = extra[frames * (levels - 1) : frames * (2 * levels - 1)]
    in_head = (jnp.arange(width)[:, None] // DHEAD == jnp.arange(width // DHEAD)[None, :]).astype(
        jnp.float32
    )
    grad_mixed = contract_last(masked, whole[3]).reshape(frames, levels, width)

    base = contract_last(temporal, w_in)[:, None, :]
    z = jnp.concatenate([base, base + looked.astype(jnp.float32)], axis=1).astype(jnp.bfloat16)
    z = z.reshape(frames * levels, width)
    query, key, value, probs, spread, mixed = depth_forward(z, whole, in_head, frames, levels)
    mixed = mixed.astype(jnp.bfloat16).reshape(frames * levels, width)
    depth_out = (
        z.astype(jnp.float32) + jnp.dot(mixed, whole[3], preferred_element_type=jnp.float32)
    ).astype(jnp.bfloat16)
    grads = depth_backward(grad_mixed, query, key, value, probs, spread, in_head)
    grad_base = jnp.sum(masked.astype(jnp.float32).reshape(frames, levels, width), axis=1)
    for grad, weights in zip(grads, whole[:3]):
        summed = jnp.sum(grad, axis=1).astype(jnp.bfloat16)
        grad_base = grad_base + jnp.dot(summed, weights, preferred_element_type=jnp.float32)
    temporal_grad = jnp.dot(
        grad_base.astype(jnp.bfloat16), w_in, preferred_element_type=jnp.float32
    ).astype(jnp.bfloat16)

    depth_out = depth_out.reshape(frames * levels, SECTIONS, part).transpose(1, 0, 2)
    temporal_grad = temporal_grad.reshape(frames, SECTIONS, -1).transpose(1, 0, 2)
    results = jnp.concatenate(
        [depth_out.reshape(SECTIONS, -1, HEAD), temporal_grad.reshape(SECTIONS, -1, HEAD)], axis=1
    )
    results = lax.all_to_all(results, "section", split_axis=0, concat_axis=0, tiled=True)
    mine = results[SECTIONS - 1]
    cut = frames * levels * part // HEAD
    depth_out = mine[:cut].reshape(frames, levels, part)
    temporal_grad = mine[cut:].reshape(frames, -1)
    return (new_keys[None], new_values[None], depth_out, temporal_grad)


def solution(mesh):
    return jax.shard_map(
        body,
        mesh=mesh,
        in_specs=(
            P(None, "frame"),
            P("section", None),
            P("section", None, "frame"),
            P("section", None, "frame"),
            P("section", None, "frame"),
            P("section", None, "frame"),
            P("section", None, "frame"),
            P(None, "section"),
            P(None, "section"),
            P(None, "section"),
            P(None, "section"),
            P(None, "section"),
            P("section", None),
            P("frame", None),
            P("frame"),
            P("frame", None, "section"),
        ),
        out_specs=(
            P("section", None, "frame"),
            P("section", None, "frame"),
            P("frame", None, "section"),
            P("frame", "section"),
        ),
        check_vma=False,
    )
```

```python
import jax
import jax.numpy as jnp
from jax import lax
from jax.experimental import pallas as pl
from jax.experimental.pallas import tpu as pltpu
from jax.sharding import PartitionSpec as P

HEAD = 128
CH = 64
CACHE = 256
DHEAD = 64
SECTIONS = 16
CHIPS = 16
PIECES = 8

EPSILON = 1e-05
MASKED = -1e30
BOTH = ("section", "frame")


def device_id(section, chip, core):
    return section * 2 * CHIPS + chip * 2 + core


def plane_pairs(first):
    lows = range(first, SECTIONS - 1, 2)
    groups = [
        [device_id(low + up, chip, core) for up in range(2) for chip in range(CHIPS)]
        for low in lows
        for core in range(2)
    ]
    for alone in sorted(set(range(SECTIONS)) - {low + up for low in lows for up in range(2)}):
        groups.append([device_id(alone, chip, core) for core in range(2) for chip in range(CHIPS)])
    return groups


def core_pairs():
    return [
        [device_id(section, chip, core) for core in range(2)]
        for section in range(SECTIONS)
        for chip in range(CHIPS)
    ]


def layer_kernel(
    where_ref,
    rows_ref,
    weight_ref,
    stash_k_ref,
    stash_v_ref,
    held_ref,
    next_ref,
    found_ref,
    send_ref,
):
    tick = where_ref[0]
    section = where_ref[1]
    chip = where_ref[2]
    core = where_ref[3]
    next_ref[0] = tick + 1
    next_ref[1] = section
    next_ref[2] = chip
    next_ref[3] = core
    block = tick - section
    total = jnp.zeros((CH, 3 * HEAD), jnp.float32)
    squares = jnp.zeros((CH, 2 * HEAD), jnp.float32)
    per_piece = CHIPS // PIECES
    depth = 2 * HEAD * per_piece
    for piece in range(PIECES):
        parts = []
        for at in range(piece * per_piece, (piece + 1) * per_piece):
            part = jnp.concatenate([rows_ref[0, at], rows_ref[1, at]], axis=1)
            wide = part.astype(jnp.float32)
            squares = squares + wide * wide
            parts.append(part)
        total = total + jnp.dot(
            jnp.concatenate(parts, axis=1),
            weight_ref[pl.ds(piece * depth, depth), :],
            preferred_element_type=jnp.float32,
        )
    scale_rows = lax.rsqrt(
        jnp.sum(squares, axis=1, keepdims=True) * (1.0 / (2 * CHIPS * HEAD)) + EPSILON
    )
    projected = (total * scale_rows).astype(jnp.bfloat16)
    query = projected[:, :HEAD]
    key_new = projected[:, HEAD : 2 * HEAD]
    value_new = projected[:, 2 * HEAD :]
    keys = jnp.concatenate([stash_k_ref[...], held_ref[0, :CH], key_new], axis=0)
    values = jnp.concatenate([stash_v_ref[...], held_ref[1, :CH], value_new], axis=0)
    scores = lax.dot_general(
        query, keys, (((1,), (1,)), ((), ())), preferred_element_type=jnp.float32
    ) * HEAD ** (-0.5)
    at_key = lax.broadcasted_iota(jnp.int32, scores.shape, 1)
    at_row = lax.broadcasted_iota(jnp.int32, scores.shape, 0)
    old = jnp.where(block > 0, CACHE + CH, CACHE)
    allowed = (at_key < old) | ((at_key >= CACHE + CH) & (at_key - (CACHE + CH) <= at_row))
    scores = jnp.where(allowed, scores, MASKED)
    peak = jnp.max(scores, axis=-1, keepdims=True)
    raised = jnp.exp(scores - peak)
    probs = (raised / jnp.sum(raised, axis=-1, keepdims=True)).astype(jnp.bfloat16)
    attended = jnp.dot(probs, values, preferred_element_type=jnp.float32)
    own = rows_ref[core, chip].astype(jnp.float32)
    x_out = (own + attended).astype(jnp.bfloat16)

    def keep(rows):
        found_ref[0, rows] = key_new
        found_ref[1, rows] = value_new
        found_ref[2, rows] = x_out

    early, late = pl.ds(0, CH), pl.ds(CH, CH)
    found_ref[...] = held_ref[...]
    pl.when(block == 0)(lambda: keep(early))
    pl.when(block == 2)(lambda: keep(late))
    for at in range(send_ref.shape[0]):
        send_ref[at] = x_out


def layer_step(where, rows, weight, stash_k, stash_v, held):
    vmem = pl.BlockSpec(memory_space=pltpu.VMEM)
    smem = pl.BlockSpec(memory_space=pltpu.SMEM)
    return pl.pallas_call(
        layer_kernel,
        out_shape=(
            jax.ShapeDtypeStruct(where.shape, where.dtype),
            jax.ShapeDtypeStruct(held.shape, held.dtype),
            jax.ShapeDtypeStruct((2 * CHIPS, CH, HEAD), jnp.bfloat16),
        ),
        in_specs=[smem, vmem, vmem, vmem, vmem, vmem],
        out_specs=(smem, vmem, vmem),
        input_output_aliases={5: 1},
        compiler_params=pltpu.CompilerParams(vmem_limit_bytes=16 * 1024 * 1024),
        cost_estimate=pl.CostEstimate(
            flops=2 * CH * weight.size, bytes_accessed=2 * weight.size, transcendentals=0
        ),
    )(where, rows, weight, stash_k, stash_v, held)


def contract_last(a, b):
    return lax.dot_general(a, b, (((1,), (1,)), ((), ())), preferred_element_type=jnp.float32)


def depth_forward(z, whole, in_head, frames, levels):
    width = z.shape[1]
    high = lax.Precision.HIGHEST
    heads = in_head.shape[1]
    query, key, value = (
        contract_last(z, whole[at]).reshape(frames, levels, width) for at in range(3)
    )
    pairs = (query[:, :, None, :] * key[:, None, :, :]).reshape(-1, width)
    scores = jnp.dot(pairs, in_head, precision=high).reshape(frames, levels, levels, heads)
    scores = scores * DHEAD ** (-0.5)
    causal = jnp.arange(levels)[:, None] >= jnp.arange(levels)[None, :]
    scores = jnp.where(causal[None, :, :, None], scores, MASKED)
    peak = jnp.max(scores, axis=2, keepdims=True)
    raised = jnp.exp(scores - peak)
    probs = raised / jnp.sum(raised, axis=2, keepdims=True)
    spread = jnp.dot(probs.reshape(-1, heads), in_head.T, precision=high).reshape(
        frames, levels, levels, width
    )
    mixed = jnp.sum(spread * value[:, None, :, :], axis=2)
    return query, key, value, probs, spread, mixed


def depth_backward(grad_mixed, query, key, value, probs, spread, in_head):
    frames, levels, width = query.shape
    heads = in_head.shape[1]
    high = lax.Precision.HIGHEST
    grad_value = jnp.sum(spread * grad_mixed[:, :, None, :], axis=1)
    pairs = (grad_mixed[:, :, None, :] * value[:, None, :, :]).reshape(-1, width)
    grad_probs = jnp.dot(pairs, in_head, precision=high).reshape(probs.shape)
    inner = jnp.sum(grad_probs * probs, axis=2, keepdims=True)
    grad_scores = probs * (grad_probs - inner) * DHEAD ** (-0.5)
    wide = jnp.dot(grad_scores.reshape(-1, heads), in_head.T, precision=high).reshape(
        frames, levels, levels, width
    )
    grad_query = jnp.sum(wide * key[:, None, :, :], axis=2)
    grad_key = jnp.sum(wide * query[:, :, None, :], axis=1)
    return grad_query, grad_key, grad_value


def body(
    inflow,
    gains,
    w_query,
    w_key,
    w_value,
    cache_keys,
    cache_values,
    w_depth_in,
    code_table,
    w_dquery,
    w_dkey,
    w_dvalue,
    w_dout,
    codes,
    speaker_mask,
    cotangent,
):
    section_id = lax.axis_index("section")
    frame_id = lax.axis_index("frame")
    frames, levels, part = cotangent.shape
    width = part * SECTIONS
    features = w_depth_in.shape[0]

    core = frame_id % 2
    half = part // 2
    looked = jnp.take(code_table, codes, axis=0).reshape(-1, part)
    masked = cotangent.astype(jnp.float32) * speaker_mask.astype(jnp.float32)[:, None, None]
    masked = masked.astype(jnp.bfloat16).reshape(-1, part)
    extra = jnp.concatenate([looked, masked], axis=0)
    extra = jnp.pad(extra, ((0, HEAD - extra.shape[0]), (0, 0))).T
    extra = lax.all_gather(extra, BOTH, axis=1, tiled=True, axis_index_groups=core_pairs())
    shares = jnp.concatenate(
        [
            lax.dynamic_slice_in_dim(share, core * half, half, 0)
            for share in (w_depth_in.T, w_dquery.T, w_dkey.T, w_dvalue.T, w_dout, extra)
        ],
        axis=1,
    )
    along = [
        [device_id(section, chip, at) for section in range(SECTIONS) for at in range(2)]
        for chip in range(CHIPS)
    ]
    shares = lax.all_gather(shares, BOTH, axis=0, tiled=True, axis_index_groups=along)

    gain = gains[0].astype(jnp.float32)[:, None]
    weight = jnp.concatenate([w_query[0], w_key[0], w_value[0]], axis=1)
    weight = (weight.astype(jnp.float32) * gain).astype(jnp.bfloat16)
    stash_k, stash_v = cache_keys[0], cache_values[0]

    def spread_out(block):
        return jnp.broadcast_to(block[None], (2 * CHIPS,) + block.shape)

    def pass_on(first, send):
        return lax.all_to_all(
            send, BOTH, split_axis=0, concat_axis=0, tiled=True, axis_index_groups=plane_pairs(first)
        )

    def layer(where, got, held):
        rows = lax.all_gather(got, BOTH, axis=0, axis_index_groups=core_pairs())
        return layer_step(where, rows, weight, stash_k, stash_v, held)

    where = jnp.stack([jnp.int32(0), section_id, frame_id // 2, core]).astype(jnp.int32)
    held = jnp.zeros((3, 2 * CH, HEAD), jnp.bfloat16)
    entry = pass_on(0, spread_out(jnp.where(section_id % 2 == 0, inflow[:CH], inflow[CH:])))
    second = entry[CHIPS:]
    where, held, send = layer(where, entry[:CHIPS], held)
    for tick in range(1, SECTIONS + 2):
        got = pass_on((tick - 1) % 2, send)[:CHIPS]
        if tick == 2:
            got = jnp.where(section_id == 0, second, got)
        where, held, send = layer(where, got, held)
    new_keys, new_values, finished = held[0], held[1], held[2]

    finished = finished.reshape(2 * CHIPS, frames, HEAD)
    temporal = lax.all_to_all(finished, "frame", split_axis=0, concat_axis=0, tiled=True)
    temporal = temporal.transpose(1, 0, 2).reshape(frames, features)
    w_in = shares[:, :features]
    whole = [
        shares[:, features + at * width : features + (at + 1) * width] for at in range(4)
    ]
    extra = shares[:, features + 4 * width :].reshape(width, 2, HEAD)
    extra = lax.dynamic_index_in_dim(extra, core, 1, keepdims=False).T
    looked = extra[: frames * (levels - 1)].reshape(frames, levels - 1, width)
    masked = extra[frames * (levels - 1) : frames * (2 * levels - 1)]
    in_head = (jnp.arange(width)[:, None] // DHEAD == jnp.arange(width // DHEAD)[None, :]).astype(
        jnp.float32
    )
    grad_mixed = contract_last(masked, whole[3]).reshape(frames, levels, width)

    base = contract_last(temporal, w_in)[:, None, :]
    z = jnp.concatenate([base, base + looked.astype(jnp.float32)], axis=1).astype(jnp.bfloat16)
    z = z.reshape(frames * levels, width)
    query, key, value, probs, spread, mixed = depth_forward(z, whole, in_head, frames, levels)
    mixed = mixed.astype(jnp.bfloat16).reshape(frames * levels, width)
    depth_out = (
        z.astype(jnp.float32) + jnp.dot(mixed, whole[3], preferred_element_type=jnp.float32)
    ).astype(jnp.bfloat16)
    grads = depth_backward(grad_mixed, query, key, value, probs, spread, in_head)
    grad_base = jnp.sum(masked.astype(jnp.float32).reshape(frames, levels, width), axis=1)
    for grad, weights in zip(grads, whole[:3]):
        summed = jnp.sum(grad, axis=1).astype(jnp.bfloat16)
        grad_base = grad_base + jnp.dot(summed, weights, preferred_element_type=jnp.float32)
    temporal_grad = jnp.dot(
        grad_base.astype(jnp.bfloat16), w_in, preferred_element_type=jnp.float32
    ).astype(jnp.bfloat16)

    depth_out = depth_out.reshape(frames * levels, SECTIONS, part).transpose(1, 0, 2)
    temporal_grad = temporal_grad.reshape(frames, SECTIONS, -1).transpose(1, 0, 2)
    results = jnp.concatenate(
        [depth_out.reshape(SECTIONS, -1, HEAD), temporal_grad.reshape(SECTIONS, -1, HEAD)], axis=1
    )
    results = lax.all_to_all(results, "section", split_axis=0, concat_axis=0, tiled=True)
    mine = results[SECTIONS - 1]
    cut = frames * levels * part // HEAD
    depth_out = mine[:cut].reshape(frames, levels, part)
    temporal_grad = mine[cut:].reshape(frames, -1)
    return (new_keys[None], new_values[None], depth_out, temporal_grad)


def solution(mesh):
    return jax.shard_map(
        body,
        mesh=mesh,
        in_specs=(
            P(None, "frame"),
            P("section", None),
            P("section", None, "frame"),
            P("section", None, "frame"),
            P("section", None, "frame"),
            P("section", None, "frame"),
            P("section", None, "frame"),
            P(None, "section"),
            P(None, "section"),
            P(None, "section"),
            P(None, "section"),
            P(None, "section"),
            P("section", None),
            P("frame", None),
            P("frame"),
            P("frame", None, "section"),
        ),
        out_specs=(
            P("section", None, "frame"),
            P("section", None, "frame"),
            P("frame", None, "section"),
            P("frame", "section"),
        ),
        check_vma=False,
    )
```

```python
import jax
import jax.numpy as jnp
from jax import lax
from jax.experimental import pallas as pl
from jax.experimental.pallas import tpu as pltpu
from jax.sharding import PartitionSpec as P

HEAD = 128
CH = 64
CACHE = 256
DHEAD = 64
SECTIONS = 16
CHIPS = 16
PIECES = 8

EPSILON = 1e-05
MASKED = -1e30
BOTH = ("section", "frame")


def device_id(section, chip, core):
    return section * 2 * CHIPS + chip * 2 + core


def plane_pairs(first):
    lows = range(first, SECTIONS - 1, 2)
    pairs = [
        [device_id(low + up, chip, core) for up in range(2)]
        for low in lows
        for chip in range(CHIPS)
        for core in range(2)
    ]
    for alone in sorted(set(range(SECTIONS)) - {low + up for low in lows for up in range(2)}):
        pairs += [[device_id(alone, chip, core) for core in range(2)] for chip in range(CHIPS)]
    return pairs


def plane_groups():
    return [
        [device_id(section, chip, core) for chip in range(CHIPS)]
        for section in range(SECTIONS)
        for core in range(2)
    ]


def core_pairs():
    return [
        [device_id(section, chip, core) for core in range(2)]
        for section in range(SECTIONS)
        for chip in range(CHIPS)
    ]


def layer_kernel(
    where_ref,
    rows_ref,
    weight_ref,
    stash_k_ref,
    stash_v_ref,
    held_ref,
    next_ref,
    found_ref,
    send_ref,
):
    tick = where_ref[0]
    section = where_ref[1]
    chip = where_ref[2]
    core = where_ref[3]
    next_ref[0] = tick + 1
    next_ref[1] = section
    next_ref[2] = chip
    next_ref[3] = core
    block = tick - section
    total = jnp.zeros((CH, 3 * HEAD), jnp.float32)
    squares = jnp.zeros((CH, 2 * HEAD), jnp.float32)
    per_piece = CHIPS // PIECES
    depth = 2 * HEAD * per_piece
    for piece in range(PIECES):
        parts = []
        for at in range(piece * per_piece, (piece + 1) * per_piece):
            part = jnp.concatenate([rows_ref[0, at], rows_ref[1, at]], axis=1)
            wide = part.astype(jnp.float32)
            squares = squares + wide * wide
            parts.append(part)
        total = total + jnp.dot(
            jnp.concatenate(parts, axis=1),
            weight_ref[pl.ds(piece * depth, depth), :],
            preferred_element_type=jnp.float32,
        )
    scale_rows = lax.rsqrt(
        jnp.sum(squares, axis=1, keepdims=True) * (1.0 / (2 * CHIPS * HEAD)) + EPSILON
    )
    projected = (total * scale_rows).astype(jnp.bfloat16)
    query = projected[:, :HEAD]
    key_new = projected[:, HEAD : 2 * HEAD]
    value_new = projected[:, 2 * HEAD :]
    keys = jnp.concatenate([stash_k_ref[...], held_ref[0, :CH], key_new], axis=0)
    values = jnp.concatenate([stash_v_ref[...], held_ref[1, :CH], value_new], axis=0)
    scores = lax.dot_general(
        query, keys, (((1,), (1,)), ((), ())), preferred_element_type=jnp.float32
    ) * HEAD ** (-0.5)
    at_key = lax.broadcasted_iota(jnp.int32, scores.shape, 1)
    at_row = lax.broadcasted_iota(jnp.int32, scores.shape, 0)
    old = jnp.where(block > 0, CACHE + CH, CACHE)
    allowed = (at_key < old) | ((at_key >= CACHE + CH) & (at_key - (CACHE + CH) <= at_row))
    scores = jnp.where(allowed, scores, MASKED)
    peak = jnp.max(scores, axis=-1, keepdims=True)
    raised = jnp.exp(scores - peak)
    probs = (raised / jnp.sum(raised, axis=-1, keepdims=True)).astype(jnp.bfloat16)
    attended = jnp.dot(probs, values, preferred_element_type=jnp.float32)
    own = rows_ref[core, chip].astype(jnp.float32)
    x_out = (own + attended).astype(jnp.bfloat16)

    def keep(rows):
        found_ref[0, rows] = key_new
        found_ref[1, rows] = value_new
        found_ref[2, rows] = x_out

    early, late = pl.ds(0, CH), pl.ds(CH, CH)
    found_ref[...] = held_ref[...]
    pl.when(block == 0)(lambda: keep(early))
    pl.when(block == 2)(lambda: keep(late))
    send_ref[...] = x_out


def layer_step(where, rows, weight, stash_k, stash_v, held):
    vmem = pl.BlockSpec(memory_space=pltpu.VMEM)
    smem = pl.BlockSpec(memory_space=pltpu.SMEM)
    return pl.pallas_call(
        layer_kernel,
        out_shape=(
            jax.ShapeDtypeStruct(where.shape, where.dtype),
            jax.ShapeDtypeStruct(held.shape, held.dtype),
            jax.ShapeDtypeStruct((CH, HEAD), jnp.bfloat16),
        ),
        in_specs=[smem, vmem, vmem, vmem, vmem, vmem],
        out_specs=(smem, vmem, vmem),
        input_output_aliases={5: 1},
        compiler_params=pltpu.CompilerParams(vmem_limit_bytes=16 * 1024 * 1024),
        cost_estimate=pl.CostEstimate(
            flops=2 * CH * weight.size, bytes_accessed=2 * weight.size, transcendentals=0
        ),
    )(where, rows, weight, stash_k, stash_v, held)


def contract_last(a, b):
    return lax.dot_general(a, b, (((1,), (1,)), ((), ())), preferred_element_type=jnp.float32)


def depth_forward(z, whole, in_head, frames, levels):
    width = z.shape[1]
    high = lax.Precision.HIGHEST
    heads = in_head.shape[1]
    query, key, value = (
        contract_last(z, whole[at]).reshape(frames, levels, width) for at in range(3)
    )
    pairs = (query[:, :, None, :] * key[:, None, :, :]).reshape(-1, width)
    scores = jnp.dot(pairs, in_head, precision=high).reshape(frames, levels, levels, heads)
    scores = scores * DHEAD ** (-0.5)
    causal = jnp.arange(levels)[:, None] >= jnp.arange(levels)[None, :]
    scores = jnp.where(causal[None, :, :, None], scores, MASKED)
    peak = jnp.max(scores, axis=2, keepdims=True)
    raised = jnp.exp(scores - peak)
    probs = raised / jnp.sum(raised, axis=2, keepdims=True)
    spread = jnp.dot(probs.reshape(-1, heads), in_head.T, precision=high).reshape(
        frames, levels, levels, width
    )
    mixed = jnp.sum(spread * value[:, None, :, :], axis=2)
    return query, key, value, probs, spread, mixed


def depth_backward(grad_mixed, query, key, value, probs, spread, in_head):
    frames, levels, width = query.shape
    heads = in_head.shape[1]
    high = lax.Precision.HIGHEST
    grad_value = jnp.sum(spread * grad_mixed[:, :, None, :], axis=1)
    pairs = (grad_mixed[:, :, None, :] * value[:, None, :, :]).reshape(-1, width)
    grad_probs = jnp.dot(pairs, in_head, precision=high).reshape(probs.shape)
    inner = jnp.sum(grad_probs * probs, axis=2, keepdims=True)
    grad_scores = probs * (grad_probs - inner) * DHEAD ** (-0.5)
    wide = jnp.dot(grad_scores.reshape(-1, heads), in_head.T, precision=high).reshape(
        frames, levels, levels, width
    )
    grad_query = jnp.sum(wide * key[:, None, :, :], axis=2)
    grad_key = jnp.sum(wide * query[:, :, None, :], axis=1)
    return grad_query, grad_key, grad_value


def body(
    inflow,
    gains,
    w_query,
    w_key,
    w_value,
    cache_keys,
    cache_values,
    w_depth_in,
    code_table,
    w_dquery,
    w_dkey,
    w_dvalue,
    w_dout,
    codes,
    speaker_mask,
    cotangent,
):
    section_id = lax.axis_index("section")
    frame_id = lax.axis_index("frame")
    frames, levels, part = cotangent.shape
    width = part * SECTIONS
    features = w_depth_in.shape[0]

    core = frame_id % 2
    half = part // 2
    looked = jnp.take(code_table, codes, axis=0).reshape(-1, part)
    masked = cotangent.astype(jnp.float32) * speaker_mask.astype(jnp.float32)[:, None, None]
    masked = masked.astype(jnp.bfloat16).reshape(-1, part)
    extra = jnp.concatenate([looked, masked], axis=0)
    extra = jnp.pad(extra, ((0, HEAD - extra.shape[0]), (0, 0))).T
    extra = lax.all_gather(extra, BOTH, axis=1, tiled=True, axis_index_groups=core_pairs())
    shares = jnp.concatenate(
        [
            lax.dynamic_slice_in_dim(share, core * half, half, 0)
            for share in (w_depth_in.T, w_dquery.T, w_dkey.T, w_dvalue.T, w_dout, extra)
        ],
        axis=1,
    )
    along = [
        [device_id(section, chip, at) for section in range(SECTIONS) for at in range(2)]
        for chip in range(CHIPS)
    ]
    shares = lax.all_gather(shares, BOTH, axis=0, tiled=True, axis_index_groups=along)

    gain = gains[0].astype(jnp.float32)[:, None]
    weight = jnp.concatenate([w_query[0], w_key[0], w_value[0]], axis=1)
    weight = (weight.astype(jnp.float32) * gain).astype(jnp.bfloat16)
    stash_k, stash_v = cache_keys[0], cache_values[0]

    def layer(where, block, held):
        got = lax.all_to_all(
            jnp.broadcast_to(block[None], (CHIPS,) + block.shape),
            BOTH,
            split_axis=0,
            concat_axis=0,
            tiled=True,
            axis_index_groups=plane_groups(),
        )
        rows = lax.all_gather(got, BOTH, axis=0, axis_index_groups=core_pairs())
        return layer_step(where, rows, weight, stash_k, stash_v, held)

    where = jnp.stack([jnp.int32(0), section_id, frame_id // 2, core]).astype(jnp.int32)
    held = jnp.zeros((3, 2 * CH, HEAD), jnp.bfloat16)
    where, held, block = layer(where, inflow[:CH], held)
    for tick in range(1, SECTIONS + 2):
        pairs = plane_pairs((tick - 1) % 2)
        block = lax.all_gather(block, BOTH, axis=0, axis_index_groups=pairs)[0]
        if tick == 2:
            block = jnp.where(section_id == 0, inflow[CH:], block)
        where, held, block = layer(where, block, held)
    new_keys, new_values, finished = held[0], held[1], held[2]

    finished = finished.reshape(2 * CHIPS, frames, HEAD)
    temporal = lax.all_to_all(finished, "frame", split_axis=0, concat_axis=0, tiled=True)
    temporal = temporal.transpose(1, 0, 2).reshape(frames, features)
    w_in = shares[:, :features]
    whole = [
        shares[:, features + at * width : features + (at + 1) * width] for at in range(4)
    ]
    extra = shares[:, features + 4 * width :].reshape(width, 2, HEAD)
    extra = lax.dynamic_index_in_dim(extra, core, 1, keepdims=False).T
    looked = extra[: frames * (levels - 1)].reshape(frames, levels - 1, width)
    masked = extra[frames * (levels - 1) : frames * (2 * levels - 1)]
    in_head = (jnp.arange(width)[:, None] // DHEAD == jnp.arange(width // DHEAD)[None, :]).astype(
        jnp.float32
    )
    grad_mixed = contract_last(masked, whole[3]).reshape(frames, levels, width)

    base = contract_last(temporal, w_in)[:, None, :]
    z = jnp.concatenate([base, base + looked.astype(jnp.float32)], axis=1).astype(jnp.bfloat16)
    z = z.reshape(frames * levels, width)
    query, key, value, probs, spread, mixed = depth_forward(z, whole, in_head, frames, levels)
    mixed = mixed.astype(jnp.bfloat16).reshape(frames * levels, width)
    depth_out = (
        z.astype(jnp.float32) + jnp.dot(mixed, whole[3], preferred_element_type=jnp.float32)
    ).astype(jnp.bfloat16)
    grads = depth_backward(grad_mixed, query, key, value, probs, spread, in_head)
    grad_base = jnp.sum(masked.astype(jnp.float32).reshape(frames, levels, width), axis=1)
    for grad, weights in zip(grads, whole[:3]):
        summed = jnp.sum(grad, axis=1).astype(jnp.bfloat16)
        grad_base = grad_base + jnp.dot(summed, weights, preferred_element_type=jnp.float32)
    temporal_grad = jnp.dot(
        grad_base.astype(jnp.bfloat16), w_in, preferred_element_type=jnp.float32
    ).astype(jnp.bfloat16)

    depth_out = depth_out.reshape(frames * levels, SECTIONS, part).transpose(1, 0, 2)
    temporal_grad = temporal_grad.reshape(frames, SECTIONS, -1).transpose(1, 0, 2)
    results = jnp.concatenate(
        [depth_out.reshape(SECTIONS, -1, HEAD), temporal_grad.reshape(SECTIONS, -1, HEAD)], axis=1
    )
    results = lax.all_to_all(results, "section", split_axis=0, concat_axis=0, tiled=True)
    mine = results[SECTIONS - 1]
    cut = frames * levels * part // HEAD
    depth_out = mine[:cut].reshape(frames, levels, part)
    temporal_grad = mine[cut:].reshape(frames, -1)
    return (new_keys[None], new_values[None], depth_out, temporal_grad)


def solution(mesh):
    return jax.shard_map(
        body,
        mesh=mesh,
        in_specs=(
            P(None, "frame"),
            P("section", None),
            P("section", None, "frame"),
            P("section", None, "frame"),
            P("section", None, "frame"),
            P("section", None, "frame"),
            P("section", None, "frame"),
            P(None, "section"),
            P(None, "section"),
            P(None, "section"),
            P(None, "section"),
            P(None, "section"),
            P("section", None),
            P("frame", None),
            P("frame"),
            P("frame", None, "section"),
        ),
        out_specs=(
            P("section", None, "frame"),
            P("section", None, "frame"),
            P("frame", None, "section"),
            P("frame", "section"),
        ),
        check_vma=False,
    )
```

```python
import jax
import jax.numpy as jnp
from jax import lax
from jax.experimental import pallas as pl
from jax.experimental.pallas import tpu as pltpu
from jax.sharding import PartitionSpec as P

HEAD = 128
CH = 64
CACHE = 256
DHEAD = 64
LEVELS = 8
SECTIONS = 16
CHIPS = 16
PIECES = 8

EPSILON = 1e-05
MASKED = -1e30
BOTH = ("section", "frame")


def device_id(section, chip, core):
    return section * 2 * CHIPS + chip * 2 + core


def plane_pairs(first):
    lows = range(first, SECTIONS - 1, 2)
    pairs = [
        [device_id(low + up, chip, core) for up in range(2)]
        for low in lows
        for chip in range(CHIPS)
        for core in range(2)
    ]
    for alone in sorted(set(range(SECTIONS)) - {low + up for low in lows for up in range(2)}):
        pairs += [[device_id(alone, chip, core) for core in range(2)] for chip in range(CHIPS)]
    return pairs


def plane_groups():
    return [
        [device_id(section, chip, core) for chip in range(CHIPS)]
        for section in range(SECTIONS)
        for core in range(2)
    ]


def core_pairs():
    return [
        [device_id(section, chip, core) for core in range(2)]
        for section in range(SECTIONS)
        for chip in range(CHIPS)
    ]


def layer_kernel(
    where_ref,
    rows_ref,
    weight_ref,
    stash_k_ref,
    stash_v_ref,
    held_ref,
    next_ref,
    found_ref,
    send_ref,
):
    tick = where_ref[0]
    section = where_ref[1]
    chip = where_ref[2]
    core = where_ref[3]
    next_ref[0] = tick + 1
    next_ref[1] = section
    next_ref[2] = chip
    next_ref[3] = core
    block = tick - section
    total = jnp.zeros((CH, 3 * HEAD), jnp.float32)
    squares = jnp.zeros((CH, 2 * HEAD), jnp.float32)
    per_piece = CHIPS // PIECES
    depth = 2 * HEAD * per_piece
    for piece in range(PIECES):
        parts = []
        for at in range(piece * per_piece, (piece + 1) * per_piece):
            part = jnp.concatenate([rows_ref[0, at], rows_ref[1, at]], axis=1)
            wide = part.astype(jnp.float32)
            squares = squares + wide * wide
            parts.append(part)
        total = total + jnp.dot(
            jnp.concatenate(parts, axis=1),
            weight_ref[pl.ds(piece * depth, depth), :],
            preferred_element_type=jnp.float32,
        )
    scale_rows = lax.rsqrt(
        jnp.sum(squares, axis=1, keepdims=True) * (1.0 / (2 * CHIPS * HEAD)) + EPSILON
    )
    projected = (total * scale_rows).astype(jnp.bfloat16)
    query = projected[:, :HEAD]
    key_new = projected[:, HEAD : 2 * HEAD]
    value_new = projected[:, 2 * HEAD :]
    keys = jnp.concatenate([stash_k_ref[...], held_ref[0, :CH], key_new], axis=0)
    values = jnp.concatenate([stash_v_ref[...], held_ref[1, :CH], value_new], axis=0)
    scores = lax.dot_general(
        query, keys, (((1,), (1,)), ((), ())), preferred_element_type=jnp.float32
    ) * HEAD ** (-0.5)
    at_key = lax.broadcasted_iota(jnp.int32, scores.shape, 1)
    at_row = lax.broadcasted_iota(jnp.int32, scores.shape, 0)
    old = jnp.where(block > 0, CACHE + CH, CACHE)
    allowed = (at_key < old) | ((at_key >= CACHE + CH) & (at_key - (CACHE + CH) <= at_row))
    scores = jnp.where(allowed, scores, MASKED)
    peak = jnp.max(scores, axis=-1, keepdims=True)
    raised = jnp.exp(scores - peak)
    probs = (raised / jnp.sum(raised, axis=-1, keepdims=True)).astype(jnp.bfloat16)
    attended = jnp.dot(probs, values, preferred_element_type=jnp.float32)
    own = rows_ref[core, chip].astype(jnp.float32)
    x_out = (own + attended).astype(jnp.bfloat16)

    def keep(rows):
        found_ref[0, rows] = key_new
        found_ref[1, rows] = value_new
        found_ref[2, rows] = x_out

    early, late = pl.ds(0, CH), pl.ds(CH, CH)
    found_ref[...] = held_ref[...]
    pl.when(block == 0)(lambda: keep(early))
    pl.when(block == 2)(lambda: keep(late))
    send_ref[...] = x_out


def layer_step(where, rows, weight, stash_k, stash_v, held):
    vmem = pl.BlockSpec(memory_space=pltpu.VMEM)
    smem = pl.BlockSpec(memory_space=pltpu.SMEM)
    return pl.pallas_call(
        layer_kernel,
        out_shape=(
            jax.ShapeDtypeStruct(where.shape, where.dtype),
            jax.ShapeDtypeStruct(held.shape, held.dtype),
            jax.ShapeDtypeStruct((CH, HEAD), jnp.bfloat16),
        ),
        in_specs=[smem, vmem, vmem, vmem, vmem, vmem],
        out_specs=(smem, vmem, vmem),
        input_output_aliases={5: 1},
        compiler_params=pltpu.CompilerParams(vmem_limit_bytes=16 * 1024 * 1024),
        cost_estimate=pl.CostEstimate(
            flops=2 * CH * weight.size, bytes_accessed=2 * weight.size, transcendentals=0
        ),
    )(where, rows, weight, stash_k, stash_v, held)


def depth_kernel(
    core_ref,
    temporal_ref,
    shares_ref,
    result_ref,
    w_in,
    w_rest,
    extra,
    in_sem,
    rest_sem,
    extra_sem,
):
    width, features = w_in.shape
    frames = temporal_ref.shape[1]
    columns = 2 * HEAD
    rows = columns // LEVELS
    heads = width // DHEAD
    shift = columns // 2
    fetch_extra = pltpu.make_async_copy(
        shares_ref.at[:, pl.ds(pl.multiple_of(features + 4 * width + core_ref[0] * HEAD, HEAD), HEAD)],
        extra,
        extra_sem,
    )
    fetch_extra.start()
    fetch_rest = []
    for at in range(4):
        span = pl.ds(features + at * width, width)
        fetch_rest.append(
            pltpu.make_async_copy(shares_ref.at[:, span], w_rest.at[at], rest_sem.at[at])
        )
    fetch_in = []
    step = width // PIECES
    for piece in range(PIECES):
        span = pl.ds(piece * step, step)
        fetch_in.append(
            pltpu.make_async_copy(
                shares_ref.at[span, pl.ds(0, features)], w_in.at[span], in_sem.at[piece]
            )
        )
    fetch_rest[3].start()
    for copy in fetch_in:
        copy.start()
    for copy in fetch_rest[:3]:
        copy.start()

    def iota(shape, axis):
        return lax.broadcasted_iota(jnp.int32, shape, axis)

    def product(left, right):
        return jnp.dot(left, right, preferred_element_type=jnp.float32)

    source, target = iota((HEAD, columns), 0), iota((HEAD, columns), 1)
    distance, level = target // rows, target % LEVELS
    same = (source == target % rows).astype(jnp.bfloat16)
    behind = ((source == target % rows - distance) & (level >= distance)).astype(jnp.bfloat16)

    fetch_extra.wait()
    known = extra[...]
    own = (iota((HEAD, HEAD), 0) == iota((HEAD, HEAD), 1) + rows).astype(jnp.bfloat16)
    own = jnp.where(iota((HEAD, HEAD), 1) < rows, own, jnp.zeros_like(own))
    masked = product(known, own).astype(jnp.bfloat16)
    masked_all = product(masked, same).astype(jnp.bfloat16)
    fetch_rest[3].wait()
    w_out = w_rest[3]
    grad_mixed = product(w_out, masked_all)

    parts = []
    for at in range(2 * CHIPS):
        part = temporal_ref[at].astype(jnp.float32)
        part = jnp.broadcast_to(part[:, None, :], (frames, LEVELS, HEAD))
        parts.append(part.reshape(rows, HEAD).astype(jnp.bfloat16))
    x_rows = jnp.concatenate(parts, axis=1)
    bases = []
    for piece in range(PIECES):
        fetch_in[piece].wait()
        bases.append(
            lax.dot_general(
                w_in[pl.ds(piece * step, step), :],
                x_rows,
                (((1,), (1,)), ((), ())),
                preferred_element_type=jnp.float32,
            )
        )
    base = jnp.concatenate(bases, axis=0)
    z_narrow = (base + known[:, :rows].astype(jnp.float32)).astype(jnp.bfloat16)
    z = jnp.concatenate(
        [z_narrow.astype(jnp.float32), jnp.zeros((width, HEAD - rows), jnp.float32)], axis=1
    )
    z_low = z.astype(jnp.bfloat16)
    z_same = product(z_low, same).astype(jnp.bfloat16)
    z_behind = product(z_low, behind).astype(jnp.bfloat16)
    for copy in fetch_rest[:3]:
        copy.wait()
    query = product(w_rest[0], z_same)
    key = product(w_rest[1], z_behind)
    value = product(w_rest[2], z_behind)

    def per_head(terms):
        return jnp.sum(terms.reshape(heads, DHEAD, columns), axis=1)

    def over_heads(terms):
        return jnp.broadcast_to(terms[:, None, :], (heads, DHEAD, columns)).reshape(width, columns)

    def over_distances(terms, combine):
        terms = combine(terms, pltpu.roll(terms, shift, 1))
        terms = combine(terms, pltpu.roll(terms, shift // 2, 1))
        return combine(terms, pltpu.roll(terms, shift // 4, 1))

    at_column = iota((heads, columns), 1)
    seen = at_column % LEVELS >= at_column // rows
    scores = jnp.where(seen, per_head(query * key) * DHEAD ** (-0.5), MASKED)
    raised = jnp.exp(scores - over_distances(scores, jnp.maximum))
    probs = raised / over_distances(raised, jnp.add)
    wide_probs = over_heads(probs)
    mixed = wide_probs * value
    mixed = mixed[:, :HEAD] + mixed[:, HEAD:]
    mixed = mixed + pltpu.roll(mixed, HEAD // 2, 1)
    mixed = mixed + pltpu.roll(mixed, HEAD // 4, 1)
    both = jnp.where(iota((width, HEAD), 1) < rows, mixed, pltpu.roll(z, rows, 1)).T
    depth_out = both[rows : 2 * rows] + product(both[:rows].astype(jnp.bfloat16), w_out)
    depth_out = depth_out.astype(jnp.bfloat16).astype(jnp.float32)

    grad_probs = per_head(grad_mixed * value)
    inner = over_distances(grad_probs * probs, jnp.add)
    grad_scores = probs * (grad_probs - inner) * DHEAD ** (-0.5)
    wide_scores = over_heads(grad_scores)

    def to_frames(slot, limit):
        at, to = iota((limit, HEAD), 0), iota((limit, HEAD), 1)
        return (at % rows // LEVELS + 8 * slot == to).astype(jnp.bfloat16)

    summed = product(masked, jnp.where(iota((HEAD, HEAD), 0) < rows, to_frames(3, HEAD), 0))
    for slot, terms in enumerate((wide_scores * key, wide_scores * query, wide_probs * grad_mixed)):
        high = terms.astype(jnp.bfloat16)
        low = (terms - high.astype(jnp.float32)).astype(jnp.bfloat16)
        pick = to_frames(slot, columns)
        summed = summed + product(high, pick) + product(low, pick)
    summed = summed.T
    grad_base = summed[24:32]
    for slot in range(3):
        grad_base = grad_base + product(
            summed[8 * slot : 8 * slot + 8].astype(jnp.bfloat16), w_rest[slot]
        )
    grad = product(grad_base.astype(jnp.bfloat16), w_in[...])

    left = iota((rows // 2, HEAD), 1) < DHEAD
    share = features // SECTIONS
    for pair in range(SECTIONS // 2):
        block = depth_out[:, pair * HEAD : (pair + 1) * HEAD]
        top, bottom = block[: rows // 2], block[rows // 2 :]
        outs = (
            jnp.where(left, top, pltpu.roll(bottom, DHEAD, 1)),
            jnp.where(left, pltpu.roll(top, DHEAD, 1), bottom),
        )
        for up in range(2):
            section = 2 * pair + up
            result_ref[section, : rows // 2] = outs[up].astype(jnp.bfloat16)
            for half in range(2):
                first = section * share + half * HEAD
                result_ref[section, rows // 2 + 8 * half : rows // 2 + 8 * half + 8] = grad[
                    :, first : first + HEAD
                ].astype(jnp.bfloat16)


def depth_part(core, temporal, shares):
    width = shares.shape[0]
    features = 2 * CHIPS * HEAD
    rows = temporal.shape[1] * LEVELS
    vmem = pl.BlockSpec(memory_space=pltpu.VMEM)
    return pl.pallas_call(
        depth_kernel,
        out_shape=jax.ShapeDtypeStruct((SECTIONS, rows // 2 + 16, HEAD), jnp.bfloat16),
        in_specs=[
            pl.BlockSpec(memory_space=pltpu.SMEM),
            vmem,
            pl.BlockSpec(memory_space=pl.ANY),
        ],
        out_specs=vmem,
        scratch_shapes=[
            pltpu.VMEM((width, features), jnp.bfloat16),
            pltpu.VMEM((4, width, width), jnp.bfloat16),
            pltpu.VMEM((width, HEAD), jnp.bfloat16),
            pltpu.SemaphoreType.DMA((PIECES,)),
            pltpu.SemaphoreType.DMA((4,)),
            pltpu.SemaphoreType.DMA,
        ],
        compiler_params=pltpu.CompilerParams(vmem_limit_bytes=50 * 1024 * 1024),
        cost_estimate=pl.CostEstimate(
            flops=64 * shares.size, bytes_accessed=2 * shares.size, transcendentals=0
        ),
    )(core, temporal, shares)


def body(
    inflow,
    gains,
    w_query,
    w_key,
    w_value,
    cache_keys,
    cache_values,
    w_depth_in,
    code_table,
    w_dquery,
    w_dkey,
    w_dvalue,
    w_dout,
    codes,
    speaker_mask,
    cotangent,
):
    section_id = lax.axis_index("section")
    frame_id = lax.axis_index("frame")
    frames, levels, part = cotangent.shape

    core = frame_id % 2
    gain = gains[0].astype(jnp.float32)[:, None]
    weight = jnp.concatenate([w_query[0], w_key[0], w_value[0]], axis=1)
    weight = (weight.astype(jnp.float32) * gain).astype(jnp.bfloat16)
    stash_k, stash_v = cache_keys[0], cache_values[0]

    def layer(where, block, held):
        got = lax.all_to_all(
            jnp.broadcast_to(block[None], (CHIPS,) + block.shape),
            BOTH,
            split_axis=0,
            concat_axis=0,
            tiled=True,
            axis_index_groups=plane_groups(),
        )
        rows = lax.all_gather(got, BOTH, axis=0, axis_index_groups=core_pairs())
        return layer_step(where, rows, weight, stash_k, stash_v, held)

    where = jnp.stack([jnp.int32(0), section_id, frame_id // 2, core]).astype(jnp.int32)
    held = jnp.zeros((3, 2 * CH, HEAD), jnp.bfloat16)
    where, held, block = layer(where, inflow[:CH], held)
    half = part // 2
    late_core = where[3]
    looked = jnp.take(code_table, codes + (late_core - core), axis=0)
    looked = jnp.pad(looked, ((0, 0), (1, 0), (0, 0))).reshape(-1, part)
    masked = cotangent.astype(jnp.float32) * speaker_mask.astype(jnp.float32)[:, None, None]
    masked = masked.astype(jnp.bfloat16).reshape(-1, part)
    extra = jnp.concatenate([looked, masked], axis=0)
    extra = jnp.pad(extra, ((0, HEAD - extra.shape[0]), (0, 0))).T
    extra = lax.all_gather(extra, BOTH, axis=1, tiled=True, axis_index_groups=core_pairs())
    shares = jnp.concatenate(
        [
            lax.dynamic_slice_in_dim(share, late_core * half, half, 0)
            for share in (w_depth_in.T, w_dquery.T, w_dkey.T, w_dvalue.T, w_dout, extra)
        ],
        axis=1,
    )
    along = [
        [device_id(section, chip, at) for section in range(SECTIONS) for at in range(2)]
        for chip in range(CHIPS)
    ]
    shares = lax.all_gather(shares, BOTH, axis=0, tiled=True, axis_index_groups=along)

    for tick in range(1, SECTIONS + 2):
        pairs = plane_pairs((tick - 1) % 2)
        block = lax.all_gather(block, BOTH, axis=0, axis_index_groups=pairs)[0]
        if tick == 2:
            block = jnp.where(section_id == 0, inflow[CH:], block)
        where, held, block = layer(where, block, held)
    new_keys, new_values, finished = held[0], held[1], held[2]

    finished = finished.reshape(2 * CHIPS, frames, HEAD)
    temporal = lax.all_to_all(finished, "frame", split_axis=0, concat_axis=0, tiled=True)
    results = depth_part(where[3:], temporal, shares)
    results = lax.all_to_all(results, "section", split_axis=0, concat_axis=0, tiled=True)
    mine = results[SECTIONS - 1]
    cut = frames * levels // 2
    depth_out = jnp.concatenate([mine[:cut, :part], mine[:cut, part:]], axis=0)
    depth_out = depth_out.reshape(frames, levels, part)
    temporal_grad = jnp.concatenate([mine[cut : cut + frames], mine[cut + 8 : cut + 8 + frames]], axis=1)
    return (new_keys[None], new_values[None], depth_out, temporal_grad)


def solution(mesh):
    return jax.shard_map(
        body,
        mesh=mesh,
        in_specs=(
            P(None, "frame"),
            P("section", None),
            P("section", None, "frame"),
            P("section", None, "frame"),
            P("section", None, "frame"),
            P("section", None, "frame"),
            P("section", None, "frame"),
            P(None, "section"),
            P(None, "section"),
            P(None, "section"),
            P(None, "section"),
            P(None, "section"),
            P("section", None),
            P("frame", None),
            P("frame"),
            P("frame", None, "section"),
        ),
        out_specs=(
            P("section", None, "frame"),
            P("section", None, "frame"),
            P("frame", None, "section"),
            P("frame", "section"),
        ),
        check_vma=False,
    )
```

```python
import jax
import jax.numpy as jnp
from jax import lax
from jax.experimental import pallas as pl
from jax.experimental.pallas import tpu as pltpu
from jax.sharding import PartitionSpec as P

HEAD = 128
CH = 64
CACHE = 256
DHEAD = 64
LEVELS = 8
SECTIONS = 16
CHIPS = 16
PIECES = 8

EPSILON = 1e-05
MASKED = -1e30
BOTH = ("section", "frame")


def device_id(section, chip, core):
    return section * 2 * CHIPS + chip * 2 + core


def plane_pairs(first):
    lows = range(first, SECTIONS - 1, 2)
    pairs = [
        [device_id(low + up, chip, core) for up in range(2)]
        for low in lows
        for chip in range(CHIPS)
        for core in range(2)
    ]
    for alone in sorted(set(range(SECTIONS)) - {low + up for low in lows for up in range(2)}):
        pairs += [[device_id(alone, chip, core) for core in range(2)] for chip in range(CHIPS)]
    return pairs


def plane_groups():
    return [
        [device_id(section, chip, core) for chip in range(CHIPS)]
        for section in range(SECTIONS)
        for core in range(2)
    ]


def core_pairs():
    return [
        [device_id(section, chip, core) for core in range(2)]
        for section in range(SECTIONS)
        for chip in range(CHIPS)
    ]


def layer_kernel(
    clock_ref,
    rows_ref,
    own_ref,
    weight_ref,
    stash_k_ref,
    stash_v_ref,
    held_ref,
    next_ref,
    found_ref,
    send_ref,
):
    block = clock_ref[0, 0]
    next_ref[...] = clock_ref[...] + 1
    total = jnp.zeros((CH, 3 * HEAD), jnp.float32)
    squares = jnp.zeros((CH, 2 * HEAD), jnp.float32)
    per_piece = CHIPS // PIECES
    depth = 2 * HEAD * per_piece
    for piece in range(PIECES):
        parts = []
        for at in range(piece * per_piece, (piece + 1) * per_piece):
            part = jnp.concatenate([rows_ref[0, at], rows_ref[1, at]], axis=1)
            wide = part.astype(jnp.float32)
            squares = squares + wide * wide
            parts.append(part)
        total = total + jnp.dot(
            jnp.concatenate(parts, axis=1),
            weight_ref[pl.ds(piece * depth, depth), :],
            preferred_element_type=jnp.float32,
        )
    scale_rows = lax.rsqrt(
        jnp.sum(squares, axis=1, keepdims=True) * (1.0 / (2 * CHIPS * HEAD)) + EPSILON
    )
    projected = (total * scale_rows).astype(jnp.bfloat16)
    query = projected[:, :HEAD]
    key_new = projected[:, HEAD : 2 * HEAD]
    value_new = projected[:, 2 * HEAD :]
    keys = jnp.concatenate([stash_k_ref[...], held_ref[0, :CH], key_new], axis=0)
    values = jnp.concatenate([stash_v_ref[...], held_ref[1, :CH], value_new], axis=0)
    scores = lax.dot_general(
        query, keys, (((1,), (1,)), ((), ())), preferred_element_type=jnp.float32
    ) * HEAD ** (-0.5)
    at_key = lax.broadcasted_iota(jnp.int32, scores.shape, 1)
    at_row = lax.broadcasted_iota(jnp.int32, scores.shape, 0)
    old = jnp.where(block > 0, CACHE + CH, CACHE)
    allowed = (at_key < old) | ((at_key >= CACHE + CH) & (at_key - (CACHE + CH) <= at_row))
    scores = jnp.where(allowed, scores, MASKED)
    peak = jnp.max(scores, axis=-1, keepdims=True)
    raised = jnp.exp(scores - peak)
    probs = (raised / jnp.sum(raised, axis=-1, keepdims=True)).astype(jnp.bfloat16)
    attended = jnp.dot(probs, values, preferred_element_type=jnp.float32)
    x_out = (own_ref[...].astype(jnp.float32) + attended).astype(jnp.bfloat16)

    def keep(rows):
        found_ref[0, rows] = key_new
        found_ref[1, rows] = value_new
        found_ref[2, rows] = x_out

    early, late = pl.ds(0, CH), pl.ds(CH, CH)
    found_ref[...] = held_ref[...]
    pl.when(block == 0)(lambda: keep(early))
    pl.when(block == 2)(lambda: keep(late))
    send_ref[...] = x_out


def layer_step(clock, rows, own, weight, stash_k, stash_v, held):
    vmem = pl.BlockSpec(memory_space=pltpu.VMEM)
    return pl.pallas_call(
        layer_kernel,
        out_shape=(
            jax.ShapeDtypeStruct(clock.shape, clock.dtype),
            jax.ShapeDtypeStruct(held.shape, held.dtype),
            jax.ShapeDtypeStruct(own.shape, own.dtype),
        ),
        in_specs=[vmem] * 7,
        out_specs=(vmem, vmem, vmem),
        input_output_aliases={6: 1},
        compiler_params=pltpu.CompilerParams(vmem_limit_bytes=16 * 1024 * 1024),
        cost_estimate=pl.CostEstimate(
            flops=2 * CH * weight.size, bytes_accessed=2 * weight.size, transcendentals=0
        ),
    )(clock, rows, own, weight, stash_k, stash_v, held)


def depth_kernel(
    temporal_ref,
    in_ref,
    query_ref,
    key_ref,
    value_ref,
    out_ref,
    result_ref,
    w_in,
    w_rest,
    extra,
    in_sem,
    rest_sem,
    extra_sem,
):
    width, features = w_in.shape
    frames = temporal_ref.shape[1]
    columns = 2 * HEAD
    rows = columns // LEVELS
    heads = width // DHEAD
    shift = columns // 2
    fetch_extra = pltpu.make_async_copy(out_ref.at[:, pl.ds(width, HEAD)], extra, extra_sem)
    fetch_extra.start()
    fetch_rest = []
    for at, ref in enumerate((query_ref, key_ref, value_ref, out_ref.at[:, pl.ds(0, width)])):
        fetch_rest.append(pltpu.make_async_copy(ref, w_rest.at[at], rest_sem.at[at]))
    fetch_in = []
    step = width // PIECES
    for piece in range(PIECES):
        span = pl.ds(piece * step, step)
        fetch_in.append(pltpu.make_async_copy(in_ref.at[span], w_in.at[span], in_sem.at[piece]))
    fetch_rest[3].start()
    for copy in fetch_in:
        copy.start()
    for copy in fetch_rest[:3]:
        copy.start()

    def iota(shape, axis):
        return lax.broadcasted_iota(jnp.int32, shape, axis)

    def product(left, right):
        return jnp.dot(left, right, preferred_element_type=jnp.float32)

    source, target = iota((HEAD, columns), 0), iota((HEAD, columns), 1)
    distance, level = target // rows, target % LEVELS
    same = (source == target % rows).astype(jnp.bfloat16)
    behind = ((source == target % rows - distance) & (level >= distance)).astype(jnp.bfloat16)

    fetch_extra.wait()
    known = extra[...]
    own = (iota((HEAD, HEAD), 0) == iota((HEAD, HEAD), 1) + rows).astype(jnp.bfloat16)
    own = jnp.where(iota((HEAD, HEAD), 1) < rows, own, jnp.zeros_like(own))
    masked = product(known, own).astype(jnp.bfloat16)
    masked_all = product(masked, same).astype(jnp.bfloat16)
    fetch_rest[3].wait()
    w_out = w_rest[3]
    grad_mixed = product(w_out, masked_all)

    parts = []
    for at in range(2 * CHIPS):
        part = temporal_ref[at].astype(jnp.float32)
        part = jnp.broadcast_to(part[:, None, :], (frames, LEVELS, HEAD))
        parts.append(part.reshape(rows, HEAD).astype(jnp.bfloat16))
    x_rows = jnp.concatenate(parts, axis=1)
    bases = []
    for piece in range(PIECES):
        fetch_in[piece].wait()
        bases.append(
            lax.dot_general(
                w_in[pl.ds(piece * step, step), :],
                x_rows,
                (((1,), (1,)), ((), ())),
                preferred_element_type=jnp.float32,
            )
        )
    base = jnp.concatenate(bases, axis=0)
    z_narrow = (base + known[:, :rows].astype(jnp.float32)).astype(jnp.bfloat16)
    z = jnp.concatenate(
        [z_narrow.astype(jnp.float32), jnp.zeros((width, HEAD - rows), jnp.float32)], axis=1
    )
    z_low = z.astype(jnp.bfloat16)
    z_same = product(z_low, same).astype(jnp.bfloat16)
    z_behind = product(z_low, behind).astype(jnp.bfloat16)
    for copy in fetch_rest[:3]:
        copy.wait()
    query = product(w_rest[0], z_same)
    key = product(w_rest[1], z_behind)
    value = product(w_rest[2], z_behind)

    def per_head(terms):
        return jnp.sum(terms.reshape(heads, DHEAD, columns), axis=1)

    def over_heads(terms):
        return jnp.broadcast_to(terms[:, None, :], (heads, DHEAD, columns)).reshape(width, columns)

    def over_distances(terms, combine):
        terms = combine(terms, pltpu.roll(terms, shift, 1))
        terms = combine(terms, pltpu.roll(terms, shift // 2, 1))
        return combine(terms, pltpu.roll(terms, shift // 4, 1))

    at_column = iota((heads, columns), 1)
    seen = at_column % LEVELS >= at_column // rows
    scores = jnp.where(seen, per_head(query * key) * DHEAD ** (-0.5), MASKED)
    raised = jnp.exp(scores - over_distances(scores, jnp.maximum))
    probs = raised / over_distances(raised, jnp.add)
    wide_probs = over_heads(probs)
    mixed = wide_probs * value
    mixed = mixed[:, :HEAD] + mixed[:, HEAD:]
    mixed = mixed + pltpu.roll(mixed, HEAD // 2, 1)
    mixed = mixed + pltpu.roll(mixed, HEAD // 4, 1)
    both = jnp.where(iota((width, HEAD), 1) < rows, mixed, pltpu.roll(z, rows, 1)).T
    depth_out = both[rows : 2 * rows] + product(both[:rows].astype(jnp.bfloat16), w_out)
    depth_out = depth_out.astype(jnp.bfloat16).astype(jnp.float32)

    grad_probs = per_head(grad_mixed * value)
    inner = over_distances(grad_probs * probs, jnp.add)
    grad_scores = probs * (grad_probs - inner) * DHEAD ** (-0.5)
    wide_scores = over_heads(grad_scores)

    def to_frames(slot, limit):
        at, to = iota((limit, HEAD), 0), iota((limit, HEAD), 1)
        return (at % rows // LEVELS + 8 * slot == to).astype(jnp.bfloat16)

    summed = product(masked, jnp.where(iota((HEAD, HEAD), 0) < rows, to_frames(3, HEAD), 0))
    for slot, terms in enumerate((wide_scores * key, wide_scores * query, wide_probs * grad_mixed)):
        high = terms.astype(jnp.bfloat16)
        low = (terms - high.astype(jnp.float32)).astype(jnp.bfloat16)
        pick = to_frames(slot, columns)
        summed = summed + product(high, pick) + product(low, pick)
    summed = summed.T
    grad_base = summed[24:32]
    for slot in range(3):
        grad_base = grad_base + product(
            summed[8 * slot : 8 * slot + 8].astype(jnp.bfloat16), w_rest[slot]
        )
    grad = product(grad_base.astype(jnp.bfloat16), w_in[...])

    left = iota((rows // 2, HEAD), 1) < DHEAD
    share = features // SECTIONS
    for pair in range(SECTIONS // 2):
        block = depth_out[:, pair * HEAD : (pair + 1) * HEAD]
        top, bottom = block[: rows // 2], block[rows // 2 :]
        outs = (
            jnp.where(left, top, pltpu.roll(bottom, DHEAD, 1)),
            jnp.where(left, pltpu.roll(top, DHEAD, 1), bottom),
        )
        for up in range(2):
            section = 2 * pair + up
            result_ref[section, : rows // 2] = outs[up].astype(jnp.bfloat16)
            for half in range(2):
                first = section * share + half * HEAD
                result_ref[section, rows // 2 + 8 * half : rows // 2 + 8 * half + 8] = grad[
                    :, first : first + HEAD
                ].astype(jnp.bfloat16)


def depth_part(temporal, weights):
    width, features = weights[0].shape
    rows = temporal.shape[1] * LEVELS
    vmem = pl.BlockSpec(memory_space=pltpu.VMEM)
    read = sum(weight.size for weight in weights)
    return pl.pallas_call(
        depth_kernel,
        out_shape=jax.ShapeDtypeStruct((SECTIONS, rows // 2 + 16, HEAD), jnp.bfloat16),
        in_specs=[vmem] + [pl.BlockSpec(memory_space=pl.ANY)] * 5,
        out_specs=vmem,
        scratch_shapes=[
            pltpu.VMEM((width, features), jnp.bfloat16),
            pltpu.VMEM((4, width, width), jnp.bfloat16),
            pltpu.VMEM((width, HEAD), jnp.bfloat16),
            pltpu.SemaphoreType.DMA((PIECES,)),
            pltpu.SemaphoreType.DMA((4,)),
            pltpu.SemaphoreType.DMA,
        ],
        compiler_params=pltpu.CompilerParams(vmem_limit_bytes=50 * 1024 * 1024),
        cost_estimate=pl.CostEstimate(flops=64 * read, bytes_accessed=2 * read, transcendentals=0),
    )(temporal, *weights)


def body(
    inflow,
    gains,
    w_query,
    w_key,
    w_value,
    cache_keys,
    cache_values,
    w_depth_in,
    code_table,
    w_dquery,
    w_dkey,
    w_dvalue,
    w_dout,
    codes,
    speaker_mask,
    cotangent,
):
    section_id = lax.axis_index("section")
    frames, levels, part = cotangent.shape

    looked = jnp.take(code_table, codes, axis=0)
    looked = jnp.pad(looked, ((0, 0), (1, 0), (0, 0))).reshape(-1, part)
    masked = cotangent.astype(jnp.float32) * speaker_mask.astype(jnp.float32)[:, None, None]
    masked = masked.astype(jnp.bfloat16).reshape(-1, part)
    extra = jnp.concatenate([looked, masked], axis=0)
    extra = jnp.pad(extra, ((0, HEAD - extra.shape[0]), (0, 0))).T
    shares = (w_depth_in.T, w_dquery.T, w_dkey.T, w_dvalue.T, jnp.concatenate([w_dout, extra], axis=1))
    weights = [lax.all_gather(share, "section", axis=0, tiled=True) for share in shares]

    gain = gains[0].astype(jnp.float32)[:, None]
    weight = jnp.concatenate([w_query[0], w_key[0], w_value[0]], axis=1)
    weight = (weight.astype(jnp.float32) * gain).astype(jnp.bfloat16)
    stash_k, stash_v = cache_keys[0], cache_values[0]

    def layer(clock, block, held):
        got = lax.all_to_all(
            jnp.broadcast_to(block[None], (CHIPS,) + block.shape),
            BOTH,
            split_axis=0,
            concat_axis=0,
            tiled=True,
            axis_index_groups=plane_groups(),
        )
        rows = lax.all_gather(got, BOTH, axis=0, axis_index_groups=core_pairs())
        return layer_step(clock, rows, block, weight, stash_k, stash_v, held)

    clock = jnp.zeros((8, HEAD), jnp.int32) - section_id
    held = jnp.zeros((3, 2 * CH, HEAD), jnp.bfloat16)
    clock, held, block = layer(clock, inflow[:CH], held)
    for tick in range(1, SECTIONS + 2):
        pairs = plane_pairs((tick - 1) % 2)
        block = lax.all_gather(block, BOTH, axis=0, axis_index_groups=pairs)[0]
        if tick == 2:
            block = jnp.where(section_id == 0, inflow[CH:], block)
        clock, held, block = layer(clock, block, held)
    new_keys, new_values, finished = held[0], held[1], held[2]

    finished = finished.reshape(2 * CHIPS, frames, HEAD)
    temporal = lax.all_to_all(finished, "frame", split_axis=0, concat_axis=0, tiled=True)
    results = depth_part(temporal, weights)
    results = lax.all_to_all(results, "section", split_axis=0, concat_axis=0, tiled=True)
    mine = results[SECTIONS - 1]
    cut = frames * levels // 2
    depth_out = jnp.concatenate([mine[:cut, :part], mine[:cut, part:]], axis=0)
    depth_out = depth_out.reshape(frames, levels, part)
    temporal_grad = jnp.concatenate([mine[cut : cut + frames], mine[cut + 8 : cut + 8 + frames]], axis=1)
    return (new_keys[None], new_values[None], depth_out, temporal_grad)


def solution(mesh):
    return jax.shard_map(
        body,
        mesh=mesh,
        in_specs=(
            P(None, "frame"),
            P("section", None),
            P("section", None, "frame"),
            P("section", None, "frame"),
            P("section", None, "frame"),
            P("section", None, "frame"),
            P("section", None, "frame"),
            P(None, "section"),
            P(None, "section"),
            P(None, "section"),
            P(None, "section"),
            P(None, "section"),
            P("section", None),
            P("frame", None),
            P("frame"),
            P("frame", None, "section"),
        ),
        out_specs=(
            P("section", None, "frame"),
            P("section", None, "frame"),
            P("frame", None, "section"),
            P("frame", "section"),
        ),
        check_vma=False,
    )
```

```python
import jax
import jax.numpy as jnp
from jax import lax
from jax.experimental import pallas as pl
from jax.experimental.pallas import tpu as pltpu
from jax.sharding import PartitionSpec as P

HEAD = 128
CH = 64
CACHE = 256
DHEAD = 64
LEVELS = 8
SECTIONS = 16
CHIPS = 16
PIECES = 8

EPSILON = 1e-05
MASKED = -1e30
BOTH = ("section", "frame")


def device_id(section, chip, core):
    return section * 2 * CHIPS + chip * 2 + core


def plane_pairs(first):
    lows = range(first, SECTIONS - 1, 2)
    pairs = [
        [device_id(low + up, chip, core) for up in range(2)]
        for low in lows
        for chip in range(CHIPS)
        for core in range(2)
    ]
    for alone in sorted(set(range(SECTIONS)) - {low + up for low in lows for up in range(2)}):
        pairs += [[device_id(alone, chip, core) for core in range(2)] for chip in range(CHIPS)]
    return pairs


def plane_groups():
    return [
        [device_id(section, chip, core) for chip in range(CHIPS)]
        for section in range(SECTIONS)
        for core in range(2)
    ]


def core_pairs():
    return [
        [device_id(section, chip, core) for core in range(2)]
        for section in range(SECTIONS)
        for chip in range(CHIPS)
    ]


def layer_kernel(
    clock_ref,
    rows_ref,
    own_ref,
    weight_ref,
    stash_k_ref,
    stash_v_ref,
    held_ref,
    next_ref,
    found_ref,
    send_ref,
):
    block = clock_ref[0, 0]
    next_ref[...] = clock_ref[...] + 1
    total = jnp.zeros((CH, 3 * HEAD), jnp.float32)
    squares = jnp.zeros((CH, 2 * HEAD), jnp.float32)
    per_piece = CHIPS // PIECES
    depth = 2 * HEAD * per_piece
    for piece in range(PIECES):
        parts = []
        for at in range(piece * per_piece, (piece + 1) * per_piece):
            part = jnp.concatenate([rows_ref[0, at], rows_ref[1, at]], axis=1)
            wide = part.astype(jnp.float32)
            squares = squares + wide * wide
            parts.append(part)
        total = total + jnp.dot(
            jnp.concatenate(parts, axis=1),
            weight_ref[pl.ds(piece * depth, depth), :],
            preferred_element_type=jnp.float32,
        )
    scale_rows = lax.rsqrt(
        jnp.sum(squares, axis=1, keepdims=True) * (1.0 / (2 * CHIPS * HEAD)) + EPSILON
    )
    projected = (total * scale_rows).astype(jnp.bfloat16)
    query = projected[:, :HEAD]
    key_new = projected[:, HEAD : 2 * HEAD]
    value_new = projected[:, 2 * HEAD :]
    keys = jnp.concatenate([stash_k_ref[...], held_ref[0, :CH], key_new], axis=0)
    values = jnp.concatenate([stash_v_ref[...], held_ref[1, :CH], value_new], axis=0)
    scores = lax.dot_general(
        query, keys, (((1,), (1,)), ((), ())), preferred_element_type=jnp.float32
    ) * HEAD ** (-0.5)
    at_key = lax.broadcasted_iota(jnp.int32, scores.shape, 1)
    at_row = lax.broadcasted_iota(jnp.int32, scores.shape, 0)
    old = jnp.where(block > 0, CACHE + CH, CACHE)
    allowed = (at_key < old) | ((at_key >= CACHE + CH) & (at_key - (CACHE + CH) <= at_row))
    scores = jnp.where(allowed, scores, MASKED)
    peak = jnp.max(scores, axis=-1, keepdims=True)
    raised = jnp.exp(scores - peak)
    probs = (raised / jnp.sum(raised, axis=-1, keepdims=True)).astype(jnp.bfloat16)
    attended = jnp.dot(probs, values, preferred_element_type=jnp.float32)
    x_out = (own_ref[...].astype(jnp.float32) + attended).astype(jnp.bfloat16)

    def keep(rows):
        found_ref[0, rows] = key_new
        found_ref[1, rows] = value_new
        found_ref[2, rows] = x_out

    early, late = pl.ds(0, CH), pl.ds(CH, CH)
    found_ref[...] = held_ref[...]
    pl.when(block == 0)(lambda: keep(early))
    pl.when(block == 2)(lambda: keep(late))
    send_ref[...] = x_out


def layer_step(clock, rows, own, weight, stash_k, stash_v, held):
    vmem = pl.BlockSpec(memory_space=pltpu.VMEM)
    return pl.pallas_call(
        layer_kernel,
        out_shape=(
            jax.ShapeDtypeStruct(clock.shape, clock.dtype),
            jax.ShapeDtypeStruct(held.shape, held.dtype),
            jax.ShapeDtypeStruct(own.shape, own.dtype),
        ),
        in_specs=[vmem] * 7,
        out_specs=(vmem, vmem, vmem),
        input_output_aliases={6: 1},
        compiler_params=pltpu.CompilerParams(vmem_limit_bytes=16 * 1024 * 1024),
        cost_estimate=pl.CostEstimate(
            flops=2 * CH * weight.size, bytes_accessed=2 * weight.size, transcendentals=0
        ),
    )(clock, rows, own, weight, stash_k, stash_v, held)


def pack_kernel(
    codes_ref,
    table_ref,
    cotangent_ref,
    query_ref,
    key_ref,
    value_ref,
    out_ref,
    packed_ref,
    small,
    sems,
):
    part = out_ref.shape[0]
    copies = [
        pltpu.make_async_copy(ref, packed_ref.at[pl.ds(at * part, part)], sems.at[at])
        for at, ref in enumerate((query_ref, key_ref, value_ref, out_ref))
    ]
    for copy in copies:
        copy.start()
    rows = cotangent_ref.shape[0]
    entries = table_ref.shape[1]
    picked = lax.broadcasted_iota(jnp.int32, (entries, HEAD), 0) == codes_ref[...]
    looked = jnp.dot(
        table_ref[...], picked.astype(jnp.bfloat16), preferred_element_type=jnp.float32
    )
    wide = cotangent_ref[...].astype(jnp.float32)
    wide = jnp.concatenate([wide, jnp.zeros((rows, HEAD - part), jnp.float32)], axis=1)
    wide = jnp.concatenate([wide, jnp.zeros((HEAD - rows, HEAD), jnp.float32)], axis=0)
    lane = lax.broadcasted_iota(jnp.int32, (part, HEAD), 1)
    extra = jnp.where(lane < rows, looked, pltpu.roll(wide.T[:part], rows, 1)).astype(jnp.bfloat16)
    strips = [extra[at : at + 16] for at in range(0, part, 16)]
    strips.append(jnp.zeros((16, small.shape[1] - part // 16 * HEAD), jnp.bfloat16))
    small[...] = jnp.concatenate(strips, axis=1)
    last = pltpu.make_async_copy(small, packed_ref.at[pl.ds(4 * part, 16)], sems.at[4])
    last.start()
    for copy in copies:
        copy.wait()
    last.wait()


def pack(codes, table, cotangent, weights):
    part, width = weights[0].shape
    vmem = pl.BlockSpec(memory_space=pltpu.VMEM)
    anywhere = pl.BlockSpec(memory_space=pl.ANY)
    return pl.pallas_call(
        pack_kernel,
        out_shape=jax.ShapeDtypeStruct((4 * part + 16, width), jnp.bfloat16),
        in_specs=[vmem] * 3 + [anywhere] * 4,
        out_specs=anywhere,
        scratch_shapes=[pltpu.VMEM((16, width), jnp.bfloat16), pltpu.SemaphoreType.DMA((5,))],
        compiler_params=pltpu.CompilerParams(vmem_limit_bytes=16 * 1024 * 1024),
    )(codes, table, cotangent, *weights)


def depth_kernel(
    temporal_ref,
    mask_ref,
    in_ref,
    packed_ref,
    result_ref,
    w_in,
    w_rest,
    extra,
    in_sem,
    rest_sem,
    extra_sem,
):
    width, features = w_in.shape
    frames = temporal_ref.shape[1]
    columns = 2 * HEAD
    rows = columns // LEVELS
    heads = width // DHEAD
    shift = columns // 2
    part = width // SECTIONS
    fetch_extra = []
    for at in range(part // 16):
        fetch_extra.append(
            pltpu.make_async_copy(
                packed_ref.at[:, pl.ds(4 * part, 16), pl.ds(at * HEAD, HEAD)],
                extra.at[:, pl.ds(at * 16, 16), :],
                extra_sem.at[at],
            )
        )
    fetch_rest = []
    for at in range(4):
        fetch_rest.append(
            pltpu.make_async_copy(
                packed_ref.at[:, pl.ds(at * part, part), :], w_rest.at[at], rest_sem.at[at]
            )
        )
    fetch_in = []
    step = width // PIECES
    for piece in range(PIECES):
        span = pl.ds(piece * step, step)
        fetch_in.append(pltpu.make_async_copy(in_ref.at[span], w_in.at[span], in_sem.at[piece]))
    for copy in fetch_extra:
        copy.start()
    fetch_rest[3].start()
    for copy in fetch_in:
        copy.start()
    for copy in fetch_rest[:3]:
        copy.start()

    def rest(at):
        return w_rest[at].reshape(width, width)

    def iota(shape, axis):
        return lax.broadcasted_iota(jnp.int32, shape, axis)

    def product(left, right):
        return jnp.dot(left, right, preferred_element_type=jnp.float32)

    source, target = iota((HEAD, columns), 0), iota((HEAD, columns), 1)
    distance, level = target // rows, target % LEVELS
    same = (source == target % rows).astype(jnp.bfloat16)
    behind = ((source == target % rows - distance) & (level >= distance)).astype(jnp.bfloat16)

    for copy in fetch_extra:
        copy.wait()
    known = extra[...].reshape(width, HEAD)
    own = (iota((HEAD, HEAD), 0) == iota((HEAD, HEAD), 1) + rows).astype(jnp.bfloat16)
    own = jnp.where(iota((HEAD, HEAD), 1) < rows, own, jnp.zeros_like(own))
    masked = (product(known, own) * mask_ref[...]).astype(jnp.bfloat16)
    masked_all = product(masked, same).astype(jnp.bfloat16)
    fetch_rest[3].wait()
    w_out = rest(3)
    grad_mixed = product(w_out, masked_all)

    parts = []
    for at in range(2 * CHIPS):
        part = temporal_ref[at].astype(jnp.float32)
        part = jnp.broadcast_to(part[:, None, :], (frames, LEVELS, HEAD))
        parts.append(part.reshape(rows, HEAD).astype(jnp.bfloat16))
    x_rows = jnp.concatenate(parts, axis=1)
    bases = []
    for piece in range(PIECES):
        fetch_in[piece].wait()
        bases.append(
            lax.dot_general(
                w_in[pl.ds(piece * step, step), :],
                x_rows,
                (((1,), (1,)), ((), ())),
                preferred_element_type=jnp.float32,
            )
        )
    base = jnp.concatenate(bases, axis=0)
    z_narrow = (base + known[:, :rows].astype(jnp.float32)).astype(jnp.bfloat16)
    z = jnp.concatenate(
        [z_narrow.astype(jnp.float32), jnp.zeros((width, HEAD - rows), jnp.float32)], axis=1
    )
    z_low = z.astype(jnp.bfloat16)
    z_same = product(z_low, same).astype(jnp.bfloat16)
    z_behind = product(z_low, behind).astype(jnp.bfloat16)
    for copy in fetch_rest[:3]:
        copy.wait()
    query = product(rest(0), z_same)
    key = product(rest(1), z_behind)
    value = product(rest(2), z_behind)

    def per_head(terms):
        return jnp.sum(terms.reshape(heads, DHEAD, columns), axis=1)

    def over_heads(terms):
        return jnp.broadcast_to(terms[:, None, :], (heads, DHEAD, columns)).reshape(width, columns)

    def over_distances(terms, combine):
        terms = combine(terms, pltpu.roll(terms, shift, 1))
        terms = combine(terms, pltpu.roll(terms, shift // 2, 1))
        return combine(terms, pltpu.roll(terms, shift // 4, 1))

    at_column = iota((heads, columns), 1)
    seen = at_column % LEVELS >= at_column // rows
    scores = jnp.where(seen, per_head(query * key) * DHEAD ** (-0.5), MASKED)
    raised = jnp.exp(scores - over_distances(scores, jnp.maximum))
    probs = raised / over_distances(raised, jnp.add)
    wide_probs = over_heads(probs)
    mixed = wide_probs * value
    mixed = mixed[:, :HEAD] + mixed[:, HEAD:]
    mixed = mixed + pltpu.roll(mixed, HEAD // 2, 1)
    mixed = mixed + pltpu.roll(mixed, HEAD // 4, 1)
    both = jnp.where(iota((width, HEAD), 1) < rows, mixed, pltpu.roll(z, rows, 1)).T
    depth_out = both[rows : 2 * rows] + product(both[:rows].astype(jnp.bfloat16), w_out)
    depth_out = depth_out.astype(jnp.bfloat16).astype(jnp.float32)

    grad_probs = per_head(grad_mixed * value)
    inner = over_distances(grad_probs * probs, jnp.add)
    grad_scores = probs * (grad_probs - inner) * DHEAD ** (-0.5)
    wide_scores = over_heads(grad_scores)

    def to_frames(slot, limit):
        at, to = iota((limit, HEAD), 0), iota((limit, HEAD), 1)
        return (at % rows // LEVELS + 8 * slot == to).astype(jnp.bfloat16)

    summed = product(masked, jnp.where(iota((HEAD, HEAD), 0) < rows, to_frames(3, HEAD), 0))
    for slot, terms in enumerate((wide_scores * key, wide_scores * query, wide_probs * grad_mixed)):
        high = terms.astype(jnp.bfloat16)
        low = (terms - high.astype(jnp.float32)).astype(jnp.bfloat16)
        pick = to_frames(slot, columns)
        summed = summed + product(high, pick) + product(low, pick)
    summed = summed.T
    grad_base = summed[24:32]
    for slot in range(3):
        grad_base = grad_base + product(
            summed[8 * slot : 8 * slot + 8].astype(jnp.bfloat16), rest(slot)
        )
    grad = product(grad_base.astype(jnp.bfloat16), w_in[...])

    left = iota((rows // 2, HEAD), 1) < DHEAD
    share = features // SECTIONS
    for pair in range(SECTIONS // 2):
        block = depth_out[:, pair * HEAD : (pair + 1) * HEAD]
        top, bottom = block[: rows // 2], block[rows // 2 :]
        outs = (
            jnp.where(left, top, pltpu.roll(bottom, DHEAD, 1)),
            jnp.where(left, pltpu.roll(top, DHEAD, 1), bottom),
        )
        for up in range(2):
            section = 2 * pair + up
            result_ref[section, : rows // 2] = outs[up].astype(jnp.bfloat16)
            for half in range(2):
                first = section * share + half * HEAD
                result_ref[section, rows // 2 + 8 * half : rows // 2 + 8 * half + 8] = grad[
                    :, first : first + HEAD
                ].astype(jnp.bfloat16)


def depth_part(temporal, mask, w_in, packed):
    width, features = w_in.shape
    part = width // SECTIONS
    rows = temporal.shape[1] * LEVELS
    vmem = pl.BlockSpec(memory_space=pltpu.VMEM)
    anywhere = pl.BlockSpec(memory_space=pl.ANY)
    read = w_in.size + packed.size
    return pl.pallas_call(
        depth_kernel,
        out_shape=jax.ShapeDtypeStruct((SECTIONS, rows // 2 + 16, HEAD), jnp.bfloat16),
        in_specs=[vmem, vmem, anywhere, anywhere],
        out_specs=vmem,
        scratch_shapes=[
            pltpu.VMEM((width, features), jnp.bfloat16),
            pltpu.VMEM((4, SECTIONS, part, width), jnp.bfloat16),
            pltpu.VMEM((SECTIONS, part, HEAD), jnp.bfloat16),
            pltpu.SemaphoreType.DMA((PIECES,)),
            pltpu.SemaphoreType.DMA((4,)),
            pltpu.SemaphoreType.DMA((part // 16,)),
        ],
        compiler_params=pltpu.CompilerParams(vmem_limit_bytes=50 * 1024 * 1024),
        cost_estimate=pl.CostEstimate(flops=64 * read, bytes_accessed=2 * read, transcendentals=0),
    )(temporal, mask, w_in, packed)


def body(
    inflow,
    gains,
    w_query,
    w_key,
    w_value,
    cache_keys,
    cache_values,
    w_depth_in,
    code_table,
    w_dquery,
    w_dkey,
    w_dvalue,
    w_dout,
    codes,
    speaker_mask,
    cotangent,
):
    section_id = lax.axis_index("section")
    frames, levels, part = cotangent.shape

    rows = frames * levels
    codes = jnp.pad(codes, ((0, 0), (1, 0)), constant_values=-1).reshape(1, rows)
    codes = jnp.pad(codes, ((0, 0), (0, HEAD - rows)), constant_values=-1)
    packed = pack(
        codes,
        code_table.T,
        cotangent.reshape(rows, part),
        (w_dquery.T, w_dkey.T, w_dvalue.T, w_dout),
    )
    packed = lax.all_gather(packed, "section", axis=0)
    w_in = lax.all_gather(w_depth_in.T, "section", axis=0, tiled=True)
    mask = jnp.pad(jnp.repeat(speaker_mask.astype(jnp.float32), levels), (0, HEAD - rows))[None]

    gain = gains[0].astype(jnp.float32)[:, None]
    weight = jnp.concatenate([w_query[0], w_key[0], w_value[0]], axis=1)
    weight = (weight.astype(jnp.float32) * gain).astype(jnp.bfloat16)
    stash_k, stash_v = cache_keys[0], cache_values[0]

    def layer(clock, block, held):
        got = lax.all_to_all(
            jnp.broadcast_to(block[None], (CHIPS,) + block.shape),
            BOTH,
            split_axis=0,
            concat_axis=0,
            tiled=True,
            axis_index_groups=plane_groups(),
        )
        rows = lax.all_gather(got, BOTH, axis=0, axis_index_groups=core_pairs())
        return layer_step(clock, rows, block, weight, stash_k, stash_v, held)

    clock = jnp.zeros((8, HEAD), jnp.int32) - section_id
    held = jnp.zeros((3, 2 * CH, HEAD), jnp.bfloat16)
    clock, held, block = layer(clock, inflow[:CH], held)
    for tick in range(1, SECTIONS + 2):
        pairs = plane_pairs((tick - 1) % 2)
        block = lax.all_gather(block, BOTH, axis=0, axis_index_groups=pairs)[0]
        if tick == 2:
            block = jnp.where(section_id == 0, inflow[CH:], block)
        clock, held, block = layer(clock, block, held)
    new_keys, new_values, finished = held[0], held[1], held[2]

    finished = finished.reshape(2 * CHIPS, frames, HEAD)
    temporal = lax.all_to_all(finished, "frame", split_axis=0, concat_axis=0, tiled=True)
    results = depth_part(temporal, mask, w_in, packed)
    results = lax.all_to_all(results, "section", split_axis=0, concat_axis=0, tiled=True)
    mine = results[SECTIONS - 1]
    cut = frames * levels // 2
    depth_out = jnp.concatenate([mine[:cut, :part], mine[:cut, part:]], axis=0)
    depth_out = depth_out.reshape(frames, levels, part)
    temporal_grad = jnp.concatenate([mine[cut : cut + frames], mine[cut + 8 : cut + 8 + frames]], axis=1)
    return (new_keys[None], new_values[None], depth_out, temporal_grad)


def solution(mesh):
    return jax.shard_map(
        body,
        mesh=mesh,
        in_specs=(
            P(None, "frame"),
            P("section", None),
            P("section", None, "frame"),
            P("section", None, "frame"),
            P("section", None, "frame"),
            P("section", None, "frame"),
            P("section", None, "frame"),
            P(None, "section"),
            P(None, "section"),
            P(None, "section"),
            P(None, "section"),
            P(None, "section"),
            P("section", None),
            P("frame", None),
            P("frame"),
            P("frame", None, "section"),
        ),
        out_specs=(
            P("section", None, "frame"),
            P("section", None, "frame"),
            P("frame", None, "section"),
            P("frame", "section"),
        ),
        check_vma=False,
    )
```

```python
import jax
import jax.numpy as jnp
from jax import lax
from jax.experimental import pallas as pl
from jax.experimental.pallas import tpu as pltpu
from jax.sharding import PartitionSpec as P

HEAD = 128
CH = 64
CACHE = 256
DHEAD = 64
LEVELS = 8
SECTIONS = 16
CHIPS = 16
PIECES = 8

EPSILON = 1e-05
MASKED = -1e30
BOTH = ("section", "frame")


def device_id(section, chip, core):
    return section * 2 * CHIPS + chip * 2 + core


def plane_pairs(first):
    lows = range(first, SECTIONS - 1, 2)
    pairs = [
        [device_id(low + up, chip, core) for up in range(2)]
        for low in lows
        for chip in range(CHIPS)
        for core in range(2)
    ]
    for alone in sorted(set(range(SECTIONS)) - {low + up for low in lows for up in range(2)}):
        pairs += [[device_id(alone, chip, core) for core in range(2)] for chip in range(CHIPS)]
    return pairs


def plane_groups():
    return [
        [device_id(section, chip, core) for chip in range(CHIPS)]
        for section in range(SECTIONS)
        for core in range(2)
    ]


def core_pairs():
    return [
        [device_id(section, chip, core) for core in range(2)]
        for section in range(SECTIONS)
        for chip in range(CHIPS)
    ]


def layer_kernel(
    clock_ref,
    rows_ref,
    own_ref,
    weight_ref,
    stash_k_ref,
    stash_v_ref,
    held_ref,
    next_ref,
    found_ref,
    send_ref,
):
    block = clock_ref[0, 0]
    next_ref[...] = clock_ref[...] + 1
    total = jnp.zeros((CH, 3 * HEAD), jnp.float32)
    squares = jnp.zeros((CH, 2 * HEAD), jnp.float32)
    per_piece = CHIPS // PIECES
    depth = 2 * HEAD * per_piece
    for piece in range(PIECES):
        parts = []
        for at in range(piece * per_piece, (piece + 1) * per_piece):
            part = jnp.concatenate([rows_ref[0, at], rows_ref[1, at]], axis=1)
            wide = part.astype(jnp.float32)
            squares = squares + wide * wide
            parts.append(part)
        total = total + jnp.dot(
            jnp.concatenate(parts, axis=1),
            weight_ref[pl.ds(piece * depth, depth), :],
            preferred_element_type=jnp.float32,
        )
    scale_rows = lax.rsqrt(
        jnp.sum(squares, axis=1, keepdims=True) * (1.0 / (2 * CHIPS * HEAD)) + EPSILON
    )
    projected = (total * scale_rows).astype(jnp.bfloat16)
    query = projected[:, :HEAD]
    key_new = projected[:, HEAD : 2 * HEAD]
    value_new = projected[:, 2 * HEAD :]
    keys = jnp.concatenate([stash_k_ref[...], held_ref[0, :CH], key_new], axis=0)
    values = jnp.concatenate([stash_v_ref[...], held_ref[1, :CH], value_new], axis=0)
    scores = lax.dot_general(
        query, keys, (((1,), (1,)), ((), ())), preferred_element_type=jnp.float32
    ) * HEAD ** (-0.5)
    at_key = lax.broadcasted_iota(jnp.int32, scores.shape, 1)
    at_row = lax.broadcasted_iota(jnp.int32, scores.shape, 0)
    old = jnp.where(block > 0, CACHE + CH, CACHE)
    allowed = (at_key < old) | ((at_key >= CACHE + CH) & (at_key - (CACHE + CH) <= at_row))
    scores = jnp.where(allowed, scores, MASKED)
    peak = jnp.max(scores, axis=-1, keepdims=True)
    raised = jnp.exp(scores - peak)
    probs = (raised / jnp.sum(raised, axis=-1, keepdims=True)).astype(jnp.bfloat16)
    attended = jnp.dot(probs, values, preferred_element_type=jnp.float32)
    x_out = (own_ref[...].astype(jnp.float32) + attended).astype(jnp.bfloat16)

    def keep(rows):
        found_ref[0, rows] = key_new
        found_ref[1, rows] = value_new
        found_ref[2, rows] = x_out

    early, late = pl.ds(0, CH), pl.ds(CH, CH)
    found_ref[...] = held_ref[...]
    pl.when(block == 0)(lambda: keep(early))
    pl.when(block == 2)(lambda: keep(late))
    send_ref[...] = x_out


def layer_step(clock, rows, own, weight, stash_k, stash_v, held):
    vmem = pl.BlockSpec(memory_space=pltpu.VMEM)
    return pl.pallas_call(
        layer_kernel,
        out_shape=(
            jax.ShapeDtypeStruct(clock.shape, clock.dtype),
            jax.ShapeDtypeStruct(held.shape, held.dtype),
            jax.ShapeDtypeStruct(own.shape, own.dtype),
        ),
        in_specs=[vmem] * 7,
        out_specs=(vmem, vmem, vmem),
        input_output_aliases={6: 1},
        compiler_params=pltpu.CompilerParams(vmem_limit_bytes=16 * 1024 * 1024),
        cost_estimate=pl.CostEstimate(
            flops=2 * CH * weight.size, bytes_accessed=2 * weight.size, transcendentals=0
        ),
    )(clock, rows, own, weight, stash_k, stash_v, held)


def pack_kernel(
    codes_ref,
    table_ref,
    cotangent_ref,
    query_ref,
    key_ref,
    value_ref,
    out_ref,
    packed_ref,
    small,
    sems,
):
    part = out_ref.shape[0]
    copies = [
        pltpu.make_async_copy(ref, packed_ref.at[pl.ds(at * part, part)], sems.at[at])
        for at, ref in enumerate((query_ref, key_ref, value_ref, out_ref))
    ]
    for copy in copies:
        copy.start()
    rows = cotangent_ref.shape[0]
    entries = table_ref.shape[1]
    picked = lax.broadcasted_iota(jnp.int32, (entries, HEAD), 0) == codes_ref[:1]
    looked = jnp.dot(
        table_ref[...], picked.astype(jnp.bfloat16), preferred_element_type=jnp.float32
    )
    wide = cotangent_ref[...].astype(jnp.float32)
    wide = jnp.concatenate([wide, jnp.zeros((rows, HEAD - part), jnp.float32)], axis=1)
    wide = jnp.concatenate([wide, jnp.zeros((HEAD - rows, HEAD), jnp.float32)], axis=0)
    lane = lax.broadcasted_iota(jnp.int32, (part, HEAD), 1)
    masked = wide.T[:part] * codes_ref[1:].astype(jnp.float32)
    extra = jnp.where(lane < rows, looked, pltpu.roll(masked, rows, 1)).astype(jnp.bfloat16)
    strips = [extra[at : at + 16] for at in range(0, part, 16)]
    strips.append(jnp.zeros((16, small.shape[1] - part // 16 * HEAD), jnp.bfloat16))
    small[...] = jnp.concatenate(strips, axis=1)
    last = pltpu.make_async_copy(small, packed_ref.at[pl.ds(4 * part, 16)], sems.at[4])
    last.start()
    for copy in copies:
        copy.wait()
    last.wait()


def pack(codes, table, cotangent, weights):
    part, width = weights[0].shape
    vmem = pl.BlockSpec(memory_space=pltpu.VMEM)
    anywhere = pl.BlockSpec(memory_space=pl.ANY)
    return pl.pallas_call(
        pack_kernel,
        out_shape=jax.ShapeDtypeStruct((4 * part + 16, width), jnp.bfloat16),
        in_specs=[vmem] * 3 + [anywhere] * 4,
        out_specs=anywhere,
        scratch_shapes=[pltpu.VMEM((16, width), jnp.bfloat16), pltpu.SemaphoreType.DMA((5,))],
        compiler_params=pltpu.CompilerParams(vmem_limit_bytes=56 * 1024 * 1024),
    )(codes, table, cotangent, *weights)


def depth_kernel(
    temporal_ref,
    in_ref,
    packed_ref,
    result_ref,
    w_in,
    w_rest,
    extra,
    in_sem,
    rest_sem,
    extra_sem,
):
    width, features = w_in.shape
    frames = temporal_ref.shape[1]
    columns = 2 * HEAD
    rows = columns // LEVELS
    heads = width // DHEAD
    shift = columns // 2
    part = width // SECTIONS
    fetch_extra = []
    for at in range(part // 16):
        fetch_extra.append(
            pltpu.make_async_copy(
                packed_ref.at[:, pl.ds(4 * part, 16), pl.ds(at * HEAD, HEAD)],
                extra.at[:, pl.ds(at * 16, 16), :],
                extra_sem.at[at],
            )
        )
    fetch_rest = []
    for at in range(4):
        fetch_rest.append(
            pltpu.make_async_copy(
                packed_ref.at[:, pl.ds(at * part, part), :], w_rest.at[at], rest_sem.at[at]
            )
        )
    fetch_in = []
    step = width // PIECES
    for piece in range(PIECES):
        span = pl.ds(piece * step, step)
        fetch_in.append(pltpu.make_async_copy(in_ref.at[span], w_in.at[span], in_sem.at[piece]))
    for copy in fetch_extra:
        copy.start()
    fetch_rest[3].start()
    for copy in fetch_in:
        copy.start()
    for copy in fetch_rest[:3]:
        copy.start()

    def rest(at):
        return w_rest[at].reshape(width, width)

    def iota(shape, axis):
        return lax.broadcasted_iota(jnp.int32, shape, axis)

    def product(left, right):
        return jnp.dot(left, right, preferred_element_type=jnp.float32)

    source, target = iota((HEAD, columns), 0), iota((HEAD, columns), 1)
    distance, level = target // rows, target % LEVELS
    same = (source == target % rows).astype(jnp.bfloat16)
    behind = ((source == target % rows - distance) & (level >= distance)).astype(jnp.bfloat16)

    for copy in fetch_extra:
        copy.wait()
    known = extra[...].reshape(width, HEAD)
    own = (iota((HEAD, HEAD), 0) == iota((HEAD, HEAD), 1) + rows).astype(jnp.bfloat16)
    own = jnp.where(iota((HEAD, HEAD), 1) < rows, own, jnp.zeros_like(own))
    masked = product(known, own).astype(jnp.bfloat16)
    masked_all = product(masked, same).astype(jnp.bfloat16)
    fetch_rest[3].wait()
    w_out = rest(3)
    grad_mixed = product(w_out, masked_all)

    parts = []
    for at in range(2 * CHIPS):
        part = temporal_ref[at].astype(jnp.float32)
        part = jnp.broadcast_to(part[:, None, :], (frames, LEVELS, HEAD))
        parts.append(part.reshape(rows, HEAD).astype(jnp.bfloat16))
    x_rows = jnp.concatenate(parts, axis=1)
    bases = []
    for piece in range(PIECES):
        fetch_in[piece].wait()
        bases.append(
            lax.dot_general(
                w_in[pl.ds(piece * step, step), :],
                x_rows,
                (((1,), (1,)), ((), ())),
                preferred_element_type=jnp.float32,
            )
        )
    base = jnp.concatenate(bases, axis=0)
    z_narrow = (base + known[:, :rows].astype(jnp.float32)).astype(jnp.bfloat16)
    z = jnp.concatenate(
        [z_narrow.astype(jnp.float32), jnp.zeros((width, HEAD - rows), jnp.float32)], axis=1
    )
    z_low = z.astype(jnp.bfloat16)
    z_same = product(z_low, same).astype(jnp.bfloat16)
    z_behind = product(z_low, behind).astype(jnp.bfloat16)
    for copy in fetch_rest[:3]:
        copy.wait()
    query = product(rest(0), z_same)
    key = product(rest(1), z_behind)
    value = product(rest(2), z_behind)

    def per_head(terms):
        return jnp.sum(terms.reshape(heads, DHEAD, columns), axis=1)

    def over_heads(terms):
        return jnp.broadcast_to(terms[:, None, :], (heads, DHEAD, columns)).reshape(width, columns)

    def over_distances(terms, combine):
        terms = combine(terms, pltpu.roll(terms, shift, 1))
        terms = combine(terms, pltpu.roll(terms, shift // 2, 1))
        return combine(terms, pltpu.roll(terms, shift // 4, 1))

    at_column = iota((heads, columns), 1)
    seen = at_column % LEVELS >= at_column // rows
    scores = jnp.where(seen, per_head(query * key) * DHEAD ** (-0.5), MASKED)
    raised = jnp.exp(scores - over_distances(scores, jnp.maximum))
    probs = raised / over_distances(raised, jnp.add)
    wide_probs = over_heads(probs)
    mixed = wide_probs * value
    mixed = mixed[:, :HEAD] + mixed[:, HEAD:]
    mixed = mixed + pltpu.roll(mixed, HEAD // 2, 1)
    mixed = mixed + pltpu.roll(mixed, HEAD // 4, 1)
    both = jnp.where(iota((width, HEAD), 1) < rows, mixed, pltpu.roll(z, rows, 1)).T
    depth_out = both[rows : 2 * rows] + product(both[:rows].astype(jnp.bfloat16), w_out)
    depth_out = depth_out.astype(jnp.bfloat16).astype(jnp.float32)

    grad_probs = per_head(grad_mixed * value)
    inner = over_distances(grad_probs * probs, jnp.add)
    grad_scores = probs * (grad_probs - inner) * DHEAD ** (-0.5)
    wide_scores = over_heads(grad_scores)

    def to_frames(slot, limit):
        at, to = iota((limit, HEAD), 0), iota((limit, HEAD), 1)
        return (at % rows // LEVELS + 8 * slot == to).astype(jnp.bfloat16)

    summed = product(masked, jnp.where(iota((HEAD, HEAD), 0) < rows, to_frames(3, HEAD), 0))
    for slot, terms in enumerate((wide_scores * key, wide_scores * query, wide_probs * grad_mixed)):
        high = terms.astype(jnp.bfloat16)
        low = (terms - high.astype(jnp.float32)).astype(jnp.bfloat16)
        pick = to_frames(slot, columns)
        summed = summed + product(high, pick) + product(low, pick)
    summed = summed.T
    grad_base = summed[24:32]
    for slot in range(3):
        grad_base = grad_base + product(
            summed[8 * slot : 8 * slot + 8].astype(jnp.bfloat16), rest(slot)
        )
    grad = product(grad_base.astype(jnp.bfloat16), w_in[...])

    left = iota((rows // 2, HEAD), 1) < DHEAD
    share = features // SECTIONS
    for pair in range(SECTIONS // 2):
        block = depth_out[:, pair * HEAD : (pair + 1) * HEAD]
        top, bottom = block[: rows // 2], block[rows // 2 :]
        outs = (
            jnp.where(left, top, pltpu.roll(bottom, DHEAD, 1)),
            jnp.where(left, pltpu.roll(top, DHEAD, 1), bottom),
        )
        for up in range(2):
            section = 2 * pair + up
            result_ref[section, : rows // 2] = outs[up].astype(jnp.bfloat16)
            first = section * share
            halves = [grad[:frames, first + at : first + at + HEAD] for at in (0, HEAD)]
            result_ref[section, rows // 2 :] = jnp.concatenate(halves, axis=0).astype(jnp.bfloat16)


def depth_part(temporal, w_in, packed):
    width, features = w_in.shape
    part = width // SECTIONS
    rows = temporal.shape[1] * LEVELS
    vmem = pl.BlockSpec(memory_space=pltpu.VMEM)
    anywhere = pl.BlockSpec(memory_space=pl.ANY)
    read = w_in.size + packed.size
    return pl.pallas_call(
        depth_kernel,
        out_shape=jax.ShapeDtypeStruct((SECTIONS, rows // 2 + 8, HEAD), jnp.bfloat16),
        in_specs=[vmem, anywhere, anywhere],
        out_specs=vmem,
        scratch_shapes=[
            pltpu.VMEM((width, features), jnp.bfloat16),
            pltpu.VMEM((4, SECTIONS, part, width), jnp.bfloat16),
            pltpu.VMEM((SECTIONS, part, HEAD), jnp.bfloat16),
            pltpu.SemaphoreType.DMA((PIECES,)),
            pltpu.SemaphoreType.DMA((4,)),
            pltpu.SemaphoreType.DMA((part // 16,)),
        ],
        compiler_params=pltpu.CompilerParams(vmem_limit_bytes=50 * 1024 * 1024),
        cost_estimate=pl.CostEstimate(flops=64 * read, bytes_accessed=2 * read, transcendentals=0),
    )(temporal, w_in, packed)


def unpack_kernel(result_ref, depth_ref, grad_ref):
    mine = result_ref[SECTIONS - 1].astype(jnp.float32)
    rows, part = depth_ref.shape
    frames = grad_ref.shape[0]
    cut = rows // 2
    depth = jnp.concatenate([mine[:cut, :part], mine[:cut, part:]], axis=0)
    depth_ref[...] = depth.astype(jnp.bfloat16)
    grad = jnp.concatenate([mine[cut : cut + frames], mine[cut + frames :]], axis=1)
    grad_ref[...] = grad.astype(jnp.bfloat16)


def unpack(results, frames, part):
    vmem = pl.BlockSpec(memory_space=pltpu.VMEM)
    depth, grad = pl.pallas_call(
        unpack_kernel,
        out_shape=(
            jax.ShapeDtypeStruct((frames * LEVELS, part), jnp.bfloat16),
            jax.ShapeDtypeStruct((frames, 2 * HEAD), jnp.bfloat16),
        ),
        in_specs=[vmem],
        out_specs=(vmem, vmem),
    )(results)
    return depth.reshape(frames, LEVELS, part), grad


def body(
    inflow,
    gains,
    w_query,
    w_key,
    w_value,
    cache_keys,
    cache_values,
    w_depth_in,
    code_table,
    w_dquery,
    w_dkey,
    w_dvalue,
    w_dout,
    codes,
    speaker_mask,
    cotangent,
):
    section_id = lax.axis_index("section")
    frames, levels, part = cotangent.shape

    rows = frames * levels
    codes = jnp.pad(codes, ((0, 0), (1, 0)), constant_values=-1).reshape(1, rows)
    mask = jnp.broadcast_to(speaker_mask[:, None], (frames, levels)).reshape(1, rows)
    codes = jnp.pad(
        jnp.concatenate([codes, mask], axis=0), ((0, 0), (0, HEAD - rows)), constant_values=-1
    )
    packed = pack(
        codes,
        code_table.T,
        cotangent.reshape(rows, part),
        (w_dquery.T, w_dkey.T, w_dvalue.T, w_dout),
    )
    packed = lax.all_gather(packed, "section", axis=0)
    w_in = lax.all_gather(w_depth_in.T, "section", axis=0, tiled=True)

    gain = gains[0].astype(jnp.float32)[:, None]
    weight = jnp.concatenate([w_query[0], w_key[0], w_value[0]], axis=1)
    weight = (weight.astype(jnp.float32) * gain).astype(jnp.bfloat16)
    stash_k, stash_v = cache_keys[0], cache_values[0]

    def layer(clock, block, held):
        got = lax.all_to_all(
            jnp.broadcast_to(block[None], (CHIPS,) + block.shape),
            BOTH,
            split_axis=0,
            concat_axis=0,
            tiled=True,
            axis_index_groups=plane_groups(),
        )
        rows = lax.all_gather(got, BOTH, axis=0, axis_index_groups=core_pairs())
        return layer_step(clock, rows, block, weight, stash_k, stash_v, held)

    clock = jnp.zeros((8, HEAD), jnp.int32) - section_id
    held = jnp.zeros((3, 2 * CH, HEAD), jnp.bfloat16)
    clock, held, block = layer(clock, inflow[:CH], held)
    for tick in range(1, SECTIONS + 2):
        pairs = plane_pairs((tick - 1) % 2)
        block = lax.all_gather(block, BOTH, axis=0, axis_index_groups=pairs)[0]
        if tick == 2:
            block = jnp.where(clock[:1] == tick, inflow[CH:], block)
        clock, held, block = layer(clock, block, held)
    new_keys, new_values, finished = held[0], held[1], held[2]

    finished = finished.reshape(2 * CHIPS, frames, HEAD)
    temporal = lax.all_to_all(finished, "frame", split_axis=0, concat_axis=0, tiled=True)
    results = depth_part(temporal, w_in, packed)
    results = lax.all_to_all(results, "section", split_axis=0, concat_axis=0, tiled=True)
    depth_out, temporal_grad = unpack(results, frames, part)
    return (new_keys[None], new_values[None], depth_out, temporal_grad)


def solution(mesh):
    return jax.shard_map(
        body,
        mesh=mesh,
        in_specs=(
            P(None, "frame"),
            P("section", None),
            P("section", None, "frame"),
            P("section", None, "frame"),
            P("section", None, "frame"),
            P("section", None, "frame"),
            P("section", None, "frame"),
            P(None, "section"),
            P(None, "section"),
            P(None, "section"),
            P(None, "section"),
            P(None, "section"),
            P("section", None),
            P("frame", None),
            P("frame"),
            P("frame", None, "section"),
        ),
        out_specs=(
            P("section", None, "frame"),
            P("section", None, "frame"),
            P("frame", None, "section"),
            P("frame", "section"),
        ),
        check_vma=False,
    )
```

```python
import jax
import jax.numpy as jnp
from jax import lax
from jax.experimental import pallas as pl
from jax.experimental.pallas import tpu as pltpu
from jax.sharding import PartitionSpec as P

HEAD = 128
CH = 64
CACHE = 256
DHEAD = 64
LEVELS = 8
SECTIONS = 16
CHIPS = 16
PIECES = 8

EPSILON = 1e-05
MASKED = -1e30
BOTH = ("section", "frame")


def device_id(section, chip, core):
    return section * 2 * CHIPS + chip * 2 + core


def plane_pairs(first):
    lows = range(first, SECTIONS - 1, 2)
    pairs = [
        [device_id(low + up, chip, core) for up in range(2)]
        for low in lows
        for chip in range(CHIPS)
        for core in range(2)
    ]
    for alone in sorted(set(range(SECTIONS)) - {low + up for low in lows for up in range(2)}):
        pairs += [[device_id(alone, chip, core) for core in range(2)] for chip in range(CHIPS)]
    return pairs


def plane_groups():
    return [
        [device_id(section, chip, core) for chip in range(CHIPS)]
        for section in range(SECTIONS)
        for core in range(2)
    ]


def core_pairs():
    return [
        [device_id(section, chip, core) for core in range(2)]
        for section in range(SECTIONS)
        for chip in range(CHIPS)
    ]


def layer_kernel(
    clock_ref,
    rows_ref,
    own_ref,
    weight_ref,
    stash_k_ref,
    stash_v_ref,
    held_ref,
    next_ref,
    found_ref,
    send_ref,
):
    block = clock_ref[0, 0]
    next_ref[...] = clock_ref[...] + 1
    total = jnp.zeros((CH, 3 * HEAD), jnp.float32)
    squares = jnp.zeros((CH, 2 * HEAD), jnp.float32)
    per_piece = CHIPS // PIECES
    depth = 2 * HEAD * per_piece
    for piece in range(PIECES):
        parts = []
        for at in range(piece * per_piece, (piece + 1) * per_piece):
            part = jnp.concatenate([rows_ref[0, at], rows_ref[1, at]], axis=1)
            wide = part.astype(jnp.float32)
            squares = squares + wide * wide
            parts.append(part)
        total = total + jnp.dot(
            jnp.concatenate(parts, axis=1),
            weight_ref[pl.ds(piece * depth, depth), :],
            preferred_element_type=jnp.float32,
        )
    scale_rows = lax.rsqrt(
        jnp.sum(squares, axis=1, keepdims=True) * (1.0 / (2 * CHIPS * HEAD)) + EPSILON
    )
    projected = (total * scale_rows).astype(jnp.bfloat16)
    query = projected[:, :HEAD]
    key_new = projected[:, HEAD : 2 * HEAD]
    value_new = projected[:, 2 * HEAD :]
    keys = jnp.concatenate([stash_k_ref[...], held_ref[0, :CH], key_new], axis=0)
    values = jnp.concatenate([stash_v_ref[...], held_ref[1, :CH], value_new], axis=0)
    scores = lax.dot_general(
        query, keys, (((1,), (1,)), ((), ())), preferred_element_type=jnp.float32
    ) * HEAD ** (-0.5)
    at_key = lax.broadcasted_iota(jnp.int32, scores.shape, 1)
    at_row = lax.broadcasted_iota(jnp.int32, scores.shape, 0)
    old = jnp.where(block > 0, CACHE + CH, CACHE)
    allowed = (at_key < old) | ((at_key >= CACHE + CH) & (at_key - (CACHE + CH) <= at_row))
    scores = jnp.where(allowed, scores, MASKED)
    peak = jnp.max(scores, axis=-1, keepdims=True)
    raised = jnp.exp(scores - peak)
    probs = (raised / jnp.sum(raised, axis=-1, keepdims=True)).astype(jnp.bfloat16)
    attended = jnp.dot(probs, values, preferred_element_type=jnp.float32)
    x_out = (own_ref[...].astype(jnp.float32) + attended).astype(jnp.bfloat16)

    def keep(rows):
        found_ref[0, rows] = key_new
        found_ref[1, rows] = value_new
        found_ref[2, rows] = x_out

    early, late = pl.ds(0, CH), pl.ds(CH, CH)
    found_ref[...] = held_ref[...]
    pl.when(block == 0)(lambda: keep(early))
    pl.when(block == 2)(lambda: keep(late))
    send_ref[...] = x_out


def layer_step(clock, rows, own, weight, stash_k, stash_v, held):
    vmem = pl.BlockSpec(memory_space=pltpu.VMEM)
    return pl.pallas_call(
        layer_kernel,
        out_shape=(
            jax.ShapeDtypeStruct(clock.shape, clock.dtype),
            jax.ShapeDtypeStruct(held.shape, held.dtype),
            jax.ShapeDtypeStruct(own.shape, own.dtype),
        ),
        in_specs=[vmem] * 7,
        out_specs=(vmem, vmem, vmem),
        input_output_aliases={6: 1},
        compiler_params=pltpu.CompilerParams(vmem_limit_bytes=16 * 1024 * 1024),
        cost_estimate=pl.CostEstimate(
            flops=2 * CH * weight.size, bytes_accessed=2 * weight.size, transcendentals=0
        ),
    )(clock, rows, own, weight, stash_k, stash_v, held)


def pack_kernel(
    codes_ref,
    mask_ref,
    table_ref,
    cotangent_ref,
    query_ref,
    key_ref,
    value_ref,
    out_ref,
    packed_ref,
    sems,
):
    part = out_ref.shape[0]
    copies = [
        pltpu.make_async_copy(ref, packed_ref.at[pl.ds(at * part, part)], sems.at[at])
        for at, ref in enumerate((query_ref, key_ref, value_ref, out_ref))
    ]
    for copy in copies:
        copy.start()
    rows = cotangent_ref.shape[0]
    entries = table_ref.shape[1]
    frames, coded = codes_ref.shape
    column = lax.broadcasted_iota(jnp.int32, (1, HEAD), 1)
    codes = jnp.full((1, HEAD), -1, jnp.int32)
    mask = jnp.zeros((1, HEAD), jnp.float32)
    for frame in range(frames):
        mask = jnp.where(column // LEVELS == frame, mask_ref[frame].astype(jnp.float32), mask)
        for at in range(coded):
            codes = jnp.where(column == frame * LEVELS + at + 1, codes_ref[frame, at], codes)
    picked = lax.broadcasted_iota(jnp.int32, (entries, HEAD), 0) == codes
    looked = jnp.dot(
        table_ref[...], picked.astype(jnp.bfloat16), preferred_element_type=jnp.float32
    )
    wide = cotangent_ref[...].astype(jnp.float32)
    wide = jnp.concatenate([wide, jnp.zeros((rows, HEAD - part), jnp.float32)], axis=1)
    wide = jnp.concatenate([wide, jnp.zeros((HEAD - rows, HEAD), jnp.float32)], axis=0)
    lane = lax.broadcasted_iota(jnp.int32, (part, HEAD), 1)
    masked = wide.T[:part] * mask
    extra = jnp.where(lane < rows, looked, pltpu.roll(masked, rows, 1)).astype(jnp.bfloat16)
    strips = [extra[at : at + 16] for at in range(0, part, 16)]
    strips.append(jnp.zeros((16, packed_ref.shape[1] - part // 16 * HEAD), jnp.bfloat16))
    packed_ref[pl.ds(4 * part, 16)] = jnp.concatenate(strips, axis=1)
    for copy in copies:
        copy.wait()


def pack(codes, mask, table, cotangent, weights):
    part, width = weights[0].shape
    vmem = pl.BlockSpec(memory_space=pltpu.VMEM)
    smem = pl.BlockSpec(memory_space=pltpu.SMEM)
    anywhere = pl.BlockSpec(memory_space=pl.ANY)
    return pl.pallas_call(
        pack_kernel,
        out_shape=jax.ShapeDtypeStruct((4 * part + 16, width), jnp.bfloat16),
        in_specs=[smem, smem, vmem, vmem] + [anywhere] * 4,
        out_specs=vmem,
        scratch_shapes=[pltpu.SemaphoreType.DMA((4,))],
        compiler_params=pltpu.CompilerParams(vmem_limit_bytes=56 * 1024 * 1024),
    )(codes, mask, table, cotangent, *weights)


def depth_kernel(
    temporal_ref,
    in_ref,
    packed_ref,
    result_ref,
    w_in,
    w_rest,
    extra,
    in_sem,
    rest_sem,
    extra_sem,
):
    width, features = w_in.shape
    frames = temporal_ref.shape[1]
    columns = 2 * HEAD
    rows = columns // LEVELS
    heads = width // DHEAD
    shift = columns // 2
    part = width // SECTIONS
    fetch_extra = []
    for at in range(part // 16):
        fetch_extra.append(
            pltpu.make_async_copy(
                packed_ref.at[:, pl.ds(4 * part, 16), pl.ds(at * HEAD, HEAD)],
                extra.at[:, pl.ds(at * 16, 16), :],
                extra_sem.at[at],
            )
        )
    fetch_rest = []
    for at in range(4):
        fetch_rest.append(
            pltpu.make_async_copy(
                packed_ref.at[:, pl.ds(at * part, part), :], w_rest.at[at], rest_sem.at[at]
            )
        )
    fetch_in = []
    step = width // PIECES
    for piece in range(PIECES):
        span = pl.ds(piece * step, step)
        fetch_in.append(pltpu.make_async_copy(in_ref.at[span], w_in.at[span], in_sem.at[piece]))
    for copy in fetch_extra:
        copy.start()
    fetch_rest[3].start()
    for copy in fetch_in:
        copy.start()
    for copy in fetch_rest[:3]:
        copy.start()

    def rest(at):
        return w_rest[at].reshape(width, width)

    def iota(shape, axis):
        return lax.broadcasted_iota(jnp.int32, shape, axis)

    def product(left, right):
        return jnp.dot(left, right, preferred_element_type=jnp.float32)

    source, target = iota((HEAD, columns), 0), iota((HEAD, columns), 1)
    distance, level = target // rows, target % LEVELS
    same = (source == target % rows).astype(jnp.bfloat16)
    behind = ((source == target % rows - distance) & (level >= distance)).astype(jnp.bfloat16)

    for copy in fetch_extra:
        copy.wait()
    known = extra[...].reshape(width, HEAD)
    own = (iota((HEAD, HEAD), 0) == iota((HEAD, HEAD), 1) + rows).astype(jnp.bfloat16)
    own = jnp.where(iota((HEAD, HEAD), 1) < rows, own, jnp.zeros_like(own))
    masked = product(known, own).astype(jnp.bfloat16)
    masked_all = product(masked, same).astype(jnp.bfloat16)
    fetch_rest[3].wait()
    w_out = rest(3)
    grad_mixed = product(w_out, masked_all)

    parts = []
    for at in range(2 * CHIPS):
        part = temporal_ref[at].astype(jnp.float32)
        part = jnp.broadcast_to(part[:, None, :], (frames, LEVELS, HEAD))
        parts.append(part.reshape(rows, HEAD).astype(jnp.bfloat16))
    x_rows = jnp.concatenate(parts, axis=1)
    bases = []
    for piece in range(PIECES):
        fetch_in[piece].wait()
        bases.append(
            lax.dot_general(
                w_in[pl.ds(piece * step, step), :],
                x_rows,
                (((1,), (1,)), ((), ())),
                preferred_element_type=jnp.float32,
            )
        )
    base = jnp.concatenate(bases, axis=0)
    z_narrow = (base + known[:, :rows].astype(jnp.float32)).astype(jnp.bfloat16)
    z = jnp.concatenate(
        [z_narrow.astype(jnp.float32), jnp.zeros((width, HEAD - rows), jnp.float32)], axis=1
    )
    z_low = z.astype(jnp.bfloat16)
    z_same = product(z_low, same).astype(jnp.bfloat16)
    z_behind = product(z_low, behind).astype(jnp.bfloat16)
    for copy in fetch_rest[:3]:
        copy.wait()
    query = product(rest(0), z_same)
    key = product(rest(1), z_behind)
    value = product(rest(2), z_behind)

    def per_head(terms):
        return jnp.sum(terms.reshape(heads, DHEAD, columns), axis=1)

    def over_heads(terms):
        return jnp.broadcast_to(terms[:, None, :], (heads, DHEAD, columns)).reshape(width, columns)

    def over_distances(terms, combine):
        terms = combine(terms, pltpu.roll(terms, shift, 1))
        terms = combine(terms, pltpu.roll(terms, shift // 2, 1))
        return combine(terms, pltpu.roll(terms, shift // 4, 1))

    at_column = iota((heads, columns), 1)
    seen = at_column % LEVELS >= at_column // rows
    scores = jnp.where(seen, per_head(query * key) * DHEAD ** (-0.5), MASKED)
    raised = jnp.exp(scores - over_distances(scores, jnp.maximum))
    probs = raised / over_distances(raised, jnp.add)
    wide_probs = over_heads(probs)
    mixed = wide_probs * value
    mixed = mixed[:, :HEAD] + mixed[:, HEAD:]
    mixed = mixed + pltpu.roll(mixed, HEAD // 2, 1)
    mixed = mixed + pltpu.roll(mixed, HEAD // 4, 1)
    both = jnp.where(iota((width, HEAD), 1) < rows, mixed, pltpu.roll(z, rows, 1)).T
    depth_out = both[rows : 2 * rows] + product(both[:rows].astype(jnp.bfloat16), w_out)
    depth_out = depth_out.astype(jnp.bfloat16).astype(jnp.float32)

    grad_probs = per_head(grad_mixed * value)
    inner = over_distances(grad_probs * probs, jnp.add)
    grad_scores = probs * (grad_probs - inner) * DHEAD ** (-0.5)
    wide_scores = over_heads(grad_scores)

    def to_frames(slot, limit):
        at, to = iota((limit, HEAD), 0), iota((limit, HEAD), 1)
        return (at % rows // LEVELS + 8 * slot == to).astype(jnp.bfloat16)

    summed = product(masked, jnp.where(iota((HEAD, HEAD), 0) < rows, to_frames(3, HEAD), 0))
    for slot, terms in enumerate((wide_scores * key, wide_scores * query, wide_probs * grad_mixed)):
        high = terms.astype(jnp.bfloat16)
        low = (terms - high.astype(jnp.float32)).astype(jnp.bfloat16)
        pick = to_frames(slot, columns)
        summed = summed + product(high, pick) + product(low, pick)
    summed = summed.T
    grad_base = summed[24:32]
    for slot in range(3):
        grad_base = grad_base + product(
            summed[8 * slot : 8 * slot + 8].astype(jnp.bfloat16), rest(slot)
        )
    grad = product(grad_base.astype(jnp.bfloat16), w_in[...])

    left = iota((rows // 2, HEAD), 1) < DHEAD
    share = features // SECTIONS
    for pair in range(SECTIONS // 2):
        block = depth_out[:, pair * HEAD : (pair + 1) * HEAD]
        top, bottom = block[: rows // 2], block[rows // 2 :]
        outs = (
            jnp.where(left, top, pltpu.roll(bottom, DHEAD, 1)),
            jnp.where(left, pltpu.roll(top, DHEAD, 1), bottom),
        )
        for up in range(2):
            section = 2 * pair + up
            result_ref[section, : rows // 2] = outs[up].astype(jnp.bfloat16)
            first = section * share
            halves = [grad[:frames, first + at : first + at + HEAD] for at in (0, HEAD)]
            result_ref[section, rows // 2 :] = jnp.concatenate(halves, axis=0).astype(jnp.bfloat16)


def depth_part(temporal, w_in, packed):
    width, features = w_in.shape
    part = width // SECTIONS
    rows = temporal.shape[1] * LEVELS
    vmem = pl.BlockSpec(memory_space=pltpu.VMEM)
    anywhere = pl.BlockSpec(memory_space=pl.ANY)
    read = w_in.size + packed.size
    return pl.pallas_call(
        depth_kernel,
        out_shape=jax.ShapeDtypeStruct((SECTIONS, rows // 2 + 8, HEAD), jnp.bfloat16),
        in_specs=[vmem, anywhere, anywhere],
        out_specs=vmem,
        scratch_shapes=[
            pltpu.VMEM((width, features), jnp.bfloat16),
            pltpu.VMEM((4, SECTIONS, part, width), jnp.bfloat16),
            pltpu.VMEM((SECTIONS, part, HEAD), jnp.bfloat16),
            pltpu.SemaphoreType.DMA((PIECES,)),
            pltpu.SemaphoreType.DMA((4,)),
            pltpu.SemaphoreType.DMA((part // 16,)),
        ],
        compiler_params=pltpu.CompilerParams(vmem_limit_bytes=50 * 1024 * 1024),
        cost_estimate=pl.CostEstimate(flops=64 * read, bytes_accessed=2 * read, transcendentals=0),
    )(temporal, w_in, packed)


def unpack_kernel(result_ref, depth_ref, grad_ref):
    mine = result_ref[SECTIONS - 1].astype(jnp.float32)
    rows, part = depth_ref.shape
    frames = grad_ref.shape[0]
    cut = rows // 2
    depth = jnp.concatenate([mine[:cut, :part], mine[:cut, part:]], axis=0)
    depth_ref[...] = depth.astype(jnp.bfloat16)
    grad = jnp.concatenate([mine[cut : cut + frames], mine[cut + frames :]], axis=1)
    grad_ref[...] = grad.astype(jnp.bfloat16)


def unpack(results, frames, part):
    vmem = pl.BlockSpec(memory_space=pltpu.VMEM)
    depth, grad = pl.pallas_call(
        unpack_kernel,
        out_shape=(
            jax.ShapeDtypeStruct((frames * LEVELS, part), jnp.bfloat16),
            jax.ShapeDtypeStruct((frames, 2 * HEAD), jnp.bfloat16),
        ),
        in_specs=[vmem],
        out_specs=(vmem, vmem),
    )(results)
    return depth.reshape(frames, LEVELS, part), grad


def body(
    inflow,
    gains,
    w_query,
    w_key,
    w_value,
    cache_keys,
    cache_values,
    w_depth_in,
    code_table,
    w_dquery,
    w_dkey,
    w_dvalue,
    w_dout,
    codes,
    speaker_mask,
    cotangent,
):
    section_id = lax.axis_index("section")
    frames, levels, part = cotangent.shape

    packed = pack(
        codes,
        speaker_mask,
        code_table.T,
        cotangent.reshape(frames * levels, part),
        (w_dquery.T, w_dkey.T, w_dvalue.T, w_dout),
    )
    packed = lax.all_gather(packed, "section", axis=0)
    w_in = lax.all_gather(w_depth_in.T, "section", axis=0, tiled=True)

    gain = gains[0].astype(jnp.float32)[:, None]
    weight = jnp.concatenate([w_query[0], w_key[0], w_value[0]], axis=1)
    weight = (weight.astype(jnp.float32) * gain).astype(jnp.bfloat16)
    stash_k, stash_v = cache_keys[0], cache_values[0]

    def layer(clock, block, held):
        got = lax.all_to_all(
            jnp.broadcast_to(block[None], (CHIPS,) + block.shape),
            BOTH,
            split_axis=0,
            concat_axis=0,
            tiled=True,
            axis_index_groups=plane_groups(),
        )
        rows = lax.all_gather(got, BOTH, axis=0, axis_index_groups=core_pairs())
        return layer_step(clock, rows, block, weight, stash_k, stash_v, held)

    clock = jnp.zeros((8, HEAD), jnp.int32) - section_id
    held = jnp.zeros((3, 2 * CH, HEAD), jnp.bfloat16)
    clock, held, block = layer(clock, inflow[:CH], held)
    for tick in range(1, SECTIONS + 2):
        pairs = plane_pairs((tick - 1) % 2)
        block = lax.all_gather(block, BOTH, axis=0, axis_index_groups=pairs)[0]
        if tick == 2:
            block = jnp.where(clock[:1] == tick, inflow[CH:], block)
        clock, held, block = layer(clock, block, held)
    new_keys, new_values, finished = held[0], held[1], held[2]

    finished = finished.reshape(2 * CHIPS, frames, HEAD)
    temporal = lax.all_to_all(finished, "frame", split_axis=0, concat_axis=0, tiled=True)
    results = depth_part(temporal, w_in, packed)
    results = lax.all_to_all(results, "section", split_axis=0, concat_axis=0, tiled=True)
    depth_out, temporal_grad = unpack(results, frames, part)
    return (new_keys[None], new_values[None], depth_out, temporal_grad)


def solution(mesh):
    return jax.shard_map(
        body,
        mesh=mesh,
        in_specs=(
            P(None, "frame"),
            P("section", None),
            P("section", None, "frame"),
            P("section", None, "frame"),
            P("section", None, "frame"),
            P("section", None, "frame"),
            P("section", None, "frame"),
            P(None, "section"),
            P(None, "section"),
            P(None, "section"),
            P(None, "section"),
            P(None, "section"),
            P("section", None),
            P("frame", None),
            P("frame"),
            P("frame", None, "section"),
        ),
        out_specs=(
            P("section", None, "frame"),
            P("section", None, "frame"),
            P("frame", None, "section"),
            P("frame", "section"),
        ),
        check_vma=False,
    )
```

```python
import jax
import jax.numpy as jnp
from jax import lax
from jax.experimental import pallas as pl
from jax.experimental.pallas import tpu as pltpu
from jax.sharding import PartitionSpec as P

HEAD = 128
CH = 64
CACHE = 256
DHEAD = 64
LEVELS = 8
SECTIONS = 16
CHIPS = 16
PIECES = 8
JOINT_AFTER = 10

EPSILON = 1e-05
MASKED = -1e30
BOTH = ("section", "frame")


def device_id(section, chip, core):
    return section * 2 * CHIPS + chip * 2 + core


def plane_pairs(first):
    lows = range(first, SECTIONS - 1, 2)
    pairs = [
        [device_id(low + up, chip, core) for up in range(2)]
        for low in lows
        for chip in range(CHIPS)
        for core in range(2)
    ]
    for alone in sorted(set(range(SECTIONS)) - {low + up for low in lows for up in range(2)}):
        pairs += [[device_id(alone, chip, core) for core in range(2)] for chip in range(CHIPS)]
    return pairs


def joint_groups():
    return [
        [device_id(low + up, chip, core) for up in range(2) for chip in range(CHIPS)]
        for low in range(0, SECTIONS, 2)
        for core in range(2)
    ]


def plane_groups():
    return [
        [device_id(section, chip, core) for chip in range(CHIPS)]
        for section in range(SECTIONS)
        for core in range(2)
    ]


def core_pairs():
    return [
        [device_id(section, chip, core) for core in range(2)]
        for section in range(SECTIONS)
        for chip in range(CHIPS)
    ]


def layer_kernel(
    clock_ref,
    rows_ref,
    weight_ref,
    stash_k_ref,
    stash_v_ref,
    held_ref,
    next_ref,
    found_ref,
    send_ref,
):
    block = clock_ref[0, 0]
    first_row = lax.broadcasted_iota(jnp.int32, clock_ref.shape, 0) == 0
    next_ref[...] = clock_ref[...] + first_row.astype(jnp.int32)
    total = jnp.zeros((CH, 3 * HEAD), jnp.float32)
    squares = jnp.zeros((CH, 2 * HEAD), jnp.float32)
    per_piece = CHIPS // PIECES
    depth = 2 * HEAD * per_piece
    for piece in range(PIECES):
        parts = []
        for at in range(piece * per_piece, (piece + 1) * per_piece):
            part = jnp.concatenate([rows_ref[0, at], rows_ref[1, at]], axis=1)
            wide = part.astype(jnp.float32)
            squares = squares + wide * wide
            parts.append(part)
        total = total + jnp.dot(
            jnp.concatenate(parts, axis=1),
            weight_ref[pl.ds(piece * depth, depth), :],
            preferred_element_type=jnp.float32,
        )
    scale_rows = lax.rsqrt(
        jnp.sum(squares, axis=1, keepdims=True) * (1.0 / (2 * CHIPS * HEAD)) + EPSILON
    )
    projected = (total * scale_rows).astype(jnp.bfloat16)
    query = projected[:, :HEAD]
    key_new = projected[:, HEAD : 2 * HEAD]
    value_new = projected[:, 2 * HEAD :]
    keys = jnp.concatenate([stash_k_ref[...], held_ref[0, :CH], key_new], axis=0)
    values = jnp.concatenate([stash_v_ref[...], held_ref[1, :CH], value_new], axis=0)
    scores = lax.dot_general(
        query, keys, (((1,), (1,)), ((), ())), preferred_element_type=jnp.float32
    ) * HEAD ** (-0.5)
    at_key = lax.broadcasted_iota(jnp.int32, scores.shape, 1)
    at_row = lax.broadcasted_iota(jnp.int32, scores.shape, 0)
    old = jnp.where(block > 0, CACHE + CH, CACHE)
    allowed = (at_key < old) | ((at_key >= CACHE + CH) & (at_key - (CACHE + CH) <= at_row))
    scores = jnp.where(allowed, scores, MASKED)
    peak = jnp.max(scores, axis=-1, keepdims=True)
    raised = jnp.exp(scores - peak)
    probs = (raised / jnp.sum(raised, axis=-1, keepdims=True)).astype(jnp.bfloat16)
    attended = jnp.dot(probs, values, preferred_element_type=jnp.float32)
    own = rows_ref[clock_ref[2, 0], clock_ref[1, 0]]
    x_out = (own.astype(jnp.float32) + attended).astype(jnp.bfloat16)

    def keep(rows):
        found_ref[0, rows] = key_new
        found_ref[1, rows] = value_new
        found_ref[2, rows] = x_out

    early, late = pl.ds(0, CH), pl.ds(CH, CH)
    found_ref[...] = held_ref[...]
    pl.when(block == 0)(lambda: keep(early))
    pl.when(block == 2)(lambda: keep(late))
    send_ref[...] = x_out


def layer_step(clock, rows, weight, stash_k, stash_v, held):
    vmem = pl.BlockSpec(memory_space=pltpu.VMEM)
    return pl.pallas_call(
        layer_kernel,
        out_shape=(
            jax.ShapeDtypeStruct(clock.shape, clock.dtype),
            jax.ShapeDtypeStruct(held.shape, held.dtype),
            jax.ShapeDtypeStruct((CH, HEAD), held.dtype),
        ),
        in_specs=[vmem] * 6,
        out_specs=(vmem, vmem, vmem),
        input_output_aliases={5: 1},
        compiler_params=pltpu.CompilerParams(vmem_limit_bytes=16 * 1024 * 1024),
        cost_estimate=pl.CostEstimate(
            flops=2 * CH * weight.size, bytes_accessed=2 * weight.size, transcendentals=0
        ),
    )(clock, rows, weight, stash_k, stash_v, held)


def pack_kernel(
    codes_ref,
    mask_ref,
    table_ref,
    cotangent_ref,
    query_ref,
    key_ref,
    value_ref,
    out_ref,
    packed_ref,
    sems,
):
    part = out_ref.shape[0]
    copies = [
        pltpu.make_async_copy(ref, packed_ref.at[pl.ds(at * part, part)], sems.at[at])
        for at, ref in enumerate((query_ref, key_ref, value_ref, out_ref))
    ]
    for copy in copies:
        copy.start()
    rows = cotangent_ref.shape[0]
    entries = table_ref.shape[1]
    frames, coded = codes_ref.shape
    column = lax.broadcasted_iota(jnp.int32, (1, HEAD), 1)
    codes = jnp.full((1, HEAD), -1, jnp.int32)
    mask = jnp.zeros((1, HEAD), jnp.float32)
    for frame in range(frames):
        mask = jnp.where(column // LEVELS == frame, mask_ref[frame].astype(jnp.float32), mask)
        for at in range(coded):
            codes = jnp.where(column == frame * LEVELS + at + 1, codes_ref[frame, at], codes)
    picked = lax.broadcasted_iota(jnp.int32, (entries, HEAD), 0) == codes
    looked = jnp.dot(
        table_ref[...], picked.astype(jnp.bfloat16), preferred_element_type=jnp.float32
    )
    wide = cotangent_ref[...].astype(jnp.float32)
    wide = jnp.concatenate([wide, jnp.zeros((rows, HEAD - part), jnp.float32)], axis=1)
    wide = jnp.concatenate([wide, jnp.zeros((HEAD - rows, HEAD), jnp.float32)], axis=0)
    lane = lax.broadcasted_iota(jnp.int32, (part, HEAD), 1)
    masked = wide.T[:part] * mask
    extra = jnp.where(lane < rows, looked, pltpu.roll(masked, rows, 1)).astype(jnp.bfloat16)
    strips = [extra[at : at + 16] for at in range(0, part, 16)]
    strips.append(jnp.zeros((16, packed_ref.shape[1] - part // 16 * HEAD), jnp.bfloat16))
    packed_ref[pl.ds(4 * part, 16)] = jnp.concatenate(strips, axis=1)
    for copy in copies:
        copy.wait()


def pack(codes, mask, table, cotangent, weights):
    part, width = weights[0].shape
    vmem = pl.BlockSpec(memory_space=pltpu.VMEM)
    smem = pl.BlockSpec(memory_space=pltpu.SMEM)
    anywhere = pl.BlockSpec(memory_space=pl.ANY)
    return pl.pallas_call(
        pack_kernel,
        out_shape=jax.ShapeDtypeStruct((4 * part + 16, width), jnp.bfloat16),
        in_specs=[smem, smem, vmem, vmem] + [anywhere] * 4,
        out_specs=vmem,
        scratch_shapes=[pltpu.SemaphoreType.DMA((4,))],
        compiler_params=pltpu.CompilerParams(vmem_limit_bytes=56 * 1024 * 1024),
    )(codes, mask, table, cotangent, *weights)


def depth_kernel(
    temporal_ref,
    in_ref,
    packed_ref,
    result_ref,
    w_in,
    w_rest,
    extra,
    in_sem,
    rest_sem,
    extra_sem,
):
    width, features = w_in.shape
    frames = temporal_ref.shape[1]
    columns = 2 * HEAD
    rows = columns // LEVELS
    heads = width // DHEAD
    shift = columns // 2
    part = width // SECTIONS
    fetch_extra = []
    for at in range(part // 16):
        fetch_extra.append(
            pltpu.make_async_copy(
                packed_ref.at[:, pl.ds(4 * part, 16), pl.ds(at * HEAD, HEAD)],
                extra.at[:, pl.ds(at * 16, 16), :],
                extra_sem.at[at],
            )
        )
    fetch_rest = []
    for at in range(4):
        fetch_rest.append(
            pltpu.make_async_copy(
                packed_ref.at[:, pl.ds(at * part, part), :], w_rest.at[at], rest_sem.at[at]
            )
        )
    fetch_in = []
    step = width // PIECES
    for piece in range(PIECES):
        span = pl.ds(piece * step, step)
        fetch_in.append(pltpu.make_async_copy(in_ref.at[span], w_in.at[span], in_sem.at[piece]))
    for copy in fetch_extra:
        copy.start()
    fetch_rest[3].start()
    for copy in fetch_in:
        copy.start()
    for copy in fetch_rest[:3]:
        copy.start()

    def rest(at):
        return w_rest[at].reshape(width, width)

    def iota(shape, axis):
        return lax.broadcasted_iota(jnp.int32, shape, axis)

    def product(left, right):
        return jnp.dot(left, right, preferred_element_type=jnp.float32)

    source, target = iota((HEAD, columns), 0), iota((HEAD, columns), 1)
    distance, level = target // rows, target % LEVELS
    same = (source == target % rows).astype(jnp.bfloat16)
    behind = ((source == target % rows - distance) & (level >= distance)).astype(jnp.bfloat16)

    for copy in fetch_extra:
        copy.wait()
    known = extra[...].reshape(width, HEAD)
    own = (iota((HEAD, HEAD), 0) == iota((HEAD, HEAD), 1) + rows).astype(jnp.bfloat16)
    own = jnp.where(iota((HEAD, HEAD), 1) < rows, own, jnp.zeros_like(own))
    masked = product(known, own).astype(jnp.bfloat16)
    masked_all = product(masked, same).astype(jnp.bfloat16)
    fetch_rest[3].wait()
    w_out = rest(3)
    grad_mixed = product(w_out, masked_all)

    parts = []
    for at in range(2 * CHIPS):
        part = temporal_ref[at].astype(jnp.float32)
        part = jnp.broadcast_to(part[:, None, :], (frames, LEVELS, HEAD))
        parts.append(part.reshape(rows, HEAD).astype(jnp.bfloat16))
    x_rows = jnp.concatenate(parts, axis=1)
    bases = []
    for piece in range(PIECES):
        fetch_in[piece].wait()
        bases.append(
            lax.dot_general(
                w_in[pl.ds(piece * step, step), :],
                x_rows,
                (((1,), (1,)), ((), ())),
                preferred_element_type=jnp.float32,
            )
        )
    base = jnp.concatenate(bases, axis=0)
    z_narrow = (base + known[:, :rows].astype(jnp.float32)).astype(jnp.bfloat16)
    z = jnp.concatenate(
        [z_narrow.astype(jnp.float32), jnp.zeros((width, HEAD - rows), jnp.float32)], axis=1
    )
    z_low = z.astype(jnp.bfloat16)
    z_same = product(z_low, same).astype(jnp.bfloat16)
    z_behind = product(z_low, behind).astype(jnp.bfloat16)
    for copy in fetch_rest[:3]:
        copy.wait()
    query = product(rest(0), z_same)
    key = product(rest(1), z_behind)
    value = product(rest(2), z_behind)

    def per_head(terms):
        return jnp.sum(terms.reshape(heads, DHEAD, columns), axis=1)

    def over_heads(terms):
        return jnp.broadcast_to(terms[:, None, :], (heads, DHEAD, columns)).reshape(width, columns)

    def over_distances(terms, combine):
        terms = combine(terms, pltpu.roll(terms, shift, 1))
        terms = combine(terms, pltpu.roll(terms, shift // 2, 1))
        return combine(terms, pltpu.roll(terms, shift // 4, 1))

    at_column = iota((heads, columns), 1)
    seen = at_column % LEVELS >= at_column // rows
    scores = jnp.where(seen, per_head(query * key) * DHEAD ** (-0.5), MASKED)
    raised = jnp.exp(scores - over_distances(scores, jnp.maximum))
    probs = raised / over_distances(raised, jnp.add)
    wide_probs = over_heads(probs)
    mixed = wide_probs * value
    mixed = mixed[:, :HEAD] + mixed[:, HEAD:]
    mixed = mixed + pltpu.roll(mixed, HEAD // 2, 1)
    mixed = mixed + pltpu.roll(mixed, HEAD // 4, 1)
    both = jnp.where(iota((width, HEAD), 1) < rows, mixed, pltpu.roll(z, rows, 1)).T
    depth_out = both[rows : 2 * rows] + product(both[:rows].astype(jnp.bfloat16), w_out)
    depth_out = depth_out.astype(jnp.bfloat16).astype(jnp.float32)

    grad_probs = per_head(grad_mixed * value)
    inner = over_distances(grad_probs * probs, jnp.add)
    grad_scores = probs * (grad_probs - inner) * DHEAD ** (-0.5)
    wide_scores = over_heads(grad_scores)

    def to_frames(slot, limit):
        at, to = iota((limit, HEAD), 0), iota((limit, HEAD), 1)
        return (at % rows // LEVELS + 8 * slot == to).astype(jnp.bfloat16)

    summed = product(masked, jnp.where(iota((HEAD, HEAD), 0) < rows, to_frames(3, HEAD), 0))
    for slot, terms in enumerate((wide_scores * key, wide_scores * query, wide_probs * grad_mixed)):
        high = terms.astype(jnp.bfloat16)
        low = (terms - high.astype(jnp.float32)).astype(jnp.bfloat16)
        pick = to_frames(slot, columns)
        summed = summed + product(high, pick) + product(low, pick)
    summed = summed.T
    grad_base = summed[24:32]
    for slot in range(3):
        grad_base = grad_base + product(
            summed[8 * slot : 8 * slot + 8].astype(jnp.bfloat16), rest(slot)
        )
    grad = product(grad_base.astype(jnp.bfloat16), w_in[...])

    left = iota((rows // 2, HEAD), 1) < DHEAD
    share = features // SECTIONS
    for pair in range(SECTIONS // 2):
        block = depth_out[:, pair * HEAD : (pair + 1) * HEAD]
        top, bottom = block[: rows // 2], block[rows // 2 :]
        outs = (
            jnp.where(left, top, pltpu.roll(bottom, DHEAD, 1)),
            jnp.where(left, pltpu.roll(top, DHEAD, 1), bottom),
        )
        for up in range(2):
            section = 2 * pair + up
            result_ref[section, : rows // 2] = outs[up].astype(jnp.bfloat16)
            first = section * share
            halves = [grad[:frames, first + at : first + at + HEAD] for at in (0, HEAD)]
            result_ref[section, rows // 2 :] = jnp.concatenate(halves, axis=0).astype(jnp.bfloat16)


def depth_part(temporal, w_in, packed):
    width, features = w_in.shape
    part = width // SECTIONS
    rows = temporal.shape[1] * LEVELS
    vmem = pl.BlockSpec(memory_space=pltpu.VMEM)
    anywhere = pl.BlockSpec(memory_space=pl.ANY)
    read = w_in.size + packed.size
    return pl.pallas_call(
        depth_kernel,
        out_shape=jax.ShapeDtypeStruct((SECTIONS, rows // 2 + 8, HEAD), jnp.bfloat16),
        in_specs=[vmem, anywhere, anywhere],
        out_specs=vmem,
        scratch_shapes=[
            pltpu.VMEM((width, features), jnp.bfloat16),
            pltpu.VMEM((4, SECTIONS, part, width), jnp.bfloat16),
            pltpu.VMEM((SECTIONS, part, HEAD), jnp.bfloat16),
            pltpu.SemaphoreType.DMA((PIECES,)),
            pltpu.SemaphoreType.DMA((4,)),
            pltpu.SemaphoreType.DMA((part // 16,)),
        ],
        compiler_params=pltpu.CompilerParams(vmem_limit_bytes=50 * 1024 * 1024),
        cost_estimate=pl.CostEstimate(flops=64 * read, bytes_accessed=2 * read, transcendentals=0),
    )(temporal, w_in, packed)


def unpack_kernel(result_ref, depth_ref, grad_ref):
    mine = result_ref[SECTIONS - 1].astype(jnp.float32)
    rows, part = depth_ref.shape
    frames = grad_ref.shape[0]
    cut = rows // 2
    depth = jnp.concatenate([mine[:cut, :part], mine[:cut, part:]], axis=0)
    depth_ref[...] = depth.astype(jnp.bfloat16)
    grad = jnp.concatenate([mine[cut : cut + frames], mine[cut + frames :]], axis=1)
    grad_ref[...] = grad.astype(jnp.bfloat16)


def unpack(results, frames, part):
    vmem = pl.BlockSpec(memory_space=pltpu.VMEM)
    depth, grad = pl.pallas_call(
        unpack_kernel,
        out_shape=(
            jax.ShapeDtypeStruct((frames * LEVELS, part), jnp.bfloat16),
            jax.ShapeDtypeStruct((frames, 2 * HEAD), jnp.bfloat16),
        ),
        in_specs=[vmem],
        out_specs=(vmem, vmem),
    )(results)
    return depth.reshape(frames, LEVELS, part), grad


def body(
    inflow,
    gains,
    w_query,
    w_key,
    w_value,
    cache_keys,
    cache_values,
    w_depth_in,
    code_table,
    w_dquery,
    w_dkey,
    w_dvalue,
    w_dout,
    codes,
    speaker_mask,
    cotangent,
):
    section_id = lax.axis_index("section")
    frame_id = lax.axis_index("frame")
    frames, levels, part = cotangent.shape

    packed = pack(
        codes,
        speaker_mask,
        code_table.T,
        cotangent.reshape(frames * levels, part),
        (w_dquery.T, w_dkey.T, w_dvalue.T, w_dout),
    )
    packed = lax.all_gather(packed, "section", axis=0)
    w_in = lax.all_gather(w_depth_in.T, "section", axis=0, tiled=True)

    gain = gains[0].astype(jnp.float32)[:, None]
    weight = jnp.concatenate([w_query[0], w_key[0], w_value[0]], axis=1)
    weight = (weight.astype(jnp.float32) * gain).astype(jnp.bfloat16)
    stash_k, stash_v = cache_keys[0], cache_values[0]

    def spread(block, groups):
        copies = jnp.broadcast_to(block[None], (len(groups[0]),) + block.shape)
        return lax.all_to_all(
            copies, BOTH, split_axis=0, concat_axis=0, tiled=True, axis_index_groups=groups
        )[:CHIPS]

    def layer(clock, got, held):
        rows = lax.all_gather(got, BOTH, axis=0, axis_index_groups=core_pairs())
        return layer_step(clock, rows, weight, stash_k, stash_v, held)

    row = lax.broadcasted_iota(jnp.int32, (8, HEAD), 0)
    clock = jnp.where(row == 0, -section_id, jnp.where(row == 1, frame_id // 2, frame_id % 2))
    held = jnp.zeros((3, 2 * CH, HEAD), jnp.bfloat16)
    clock, held, block = layer(clock, spread(inflow[:CH], plane_groups()), held)
    for tick in range(1, SECTIONS + 2):
        if tick > JOINT_AFTER and tick % 2 == 1:
            got = spread(block, joint_groups())
        else:
            pairs = plane_pairs((tick - 1) % 2)
            block = lax.all_gather(block, BOTH, axis=0, axis_index_groups=pairs)[0]
            if tick == 2:
                block = jnp.where(clock[:1] == tick, inflow[CH:], block)
            got = spread(block, plane_groups())
        clock, held, block = layer(clock, got, held)
    new_keys, new_values, finished = held[0], held[1], held[2]

    finished = finished.reshape(2 * CHIPS, frames, HEAD)
    temporal = lax.all_to_all(finished, "frame", split_axis=0, concat_axis=0, tiled=True)
    results = depth_part(temporal, w_in, packed)
    results = lax.all_to_all(results, "section", split_axis=0, concat_axis=0, tiled=True)
    depth_out, temporal_grad = unpack(results, frames, part)
    return (new_keys[None], new_values[None], depth_out, temporal_grad)


def solution(mesh):
    return jax.shard_map(
        body,
        mesh=mesh,
        in_specs=(
            P(None, "frame"),
            P("section", None),
            P("section", None, "frame"),
            P("section", None, "frame"),
            P("section", None, "frame"),
            P("section", None, "frame"),
            P("section", None, "frame"),
            P(None, "section"),
            P(None, "section"),
            P(None, "section"),
            P(None, "section"),
            P(None, "section"),
            P("section", None),
            P("frame", None),
            P("frame"),
            P("frame", None, "section"),
        ),
        out_specs=(
            P("section", None, "frame"),
            P("section", None, "frame"),
            P("frame", None, "section"),
            P("frame", "section"),
        ),
        check_vma=False,
    )
```
